512 devices in a mesh: gz: 128 (over z, y, core), gy: 2 (over x_hi), gx: 2 (over x_lo).
Axes of the slice: x: 4 (x_hi: 2, x_lo: 2; x = x_hi * 2 + x_lo), y: 8, z: 8, core: 2. Of those that a mesh axis runs over, the one named last changes fastest.
Arguments:
- density: float32 [256, 512, 512], P('gz', 'gy', 'gx'), may hold values from -6 to 6
- bins: int32 [256, 512, 512], P('gz', 'gy', 'gx'), may hold values from 0 to 255
- tf_color: bfloat16 [3, 256], replicated, may hold values from 0.5 to 4
- tf_opacity: bfloat16 [1, 256], replicated, may hold values from 0.0009994507 to 0.039794922
- view_back: int32 [512], P('gx'), may hold values from 0 to 1
Outputs:
- image: float32 [4, 2, 128, 2, 512], P(None, 'gy', 'gz', None, 'gx')
The draws below stay inside these ranges and needn't reach their ends.
All inputs are finite; a program needn't handle non-finite values.
Results may differ from the reference program's by a relative error of at most 0.0003.
Values sent between devices are 32-bit elements; how exact they have to be, the bound alone decides.
A program may use at most 64 MiB of HBM per device.

```python
import math
import jax
import jax.numpy as jnp
from jax import lax

CZ = 2
TFBINS = 256
NZ = 256
NY = 512
NX = 512
FR = 2
N_GZ = 128
N_GY = 2


def draw_bins(key, part):
    key = jax.random.fold_in(key, 7)
    base_key, jitter_key = jax.random.split(key)
    slab_count = NZ // CZ
    base_bins = jax.random.randint(base_key, (slab_count, 1, NY, NX), 0, TFBINS, dtype=jnp.int32)
    jitter = jax.random.randint(jitter_key, (slab_count, CZ, NY, NX), 0, 2, dtype=jnp.int32)
    drawn = ((base_bins + jitter) % TFBINS).reshape(NZ, NY, NX)
    drawn = drawn.at[0, 0, 0].set(0)
    drawn = drawn.at[0, 0, 1].set(TFBINS - 1)
    return drawn


def touch_ends(values, stream_key, low, top_value):
    longest = values.shape.index(max(values.shape))
    spots = []
    for shift in (0, 1):
        where = [jax.random.randint(jax.random.fold_in(stream_key, axis), (), 0, length) for axis, length in enumerate(values.shape)]
        where[longest] = (where[longest] + shift) % values.shape[longest]
        spots.append(tuple(where))
    return values.at[spots[0]].set(low).at[spots[1]].set(top_value)


def shard_levels(own_key, shape, pieces, smallest, top_value):
    def one(position, blocks):
        steps = jax.random.uniform(jax.random.fold_in(jax.random.fold_in(own_key, 6), position), (blocks,), jnp.float32, smallest / len(pieces), top_value / len(pieces))
        return jnp.repeat(jnp.exp(steps), shape[position] // blocks).reshape((-1,) + (1,) * (len(shape) - position - 1))

    level = one(*pieces[0])
    for cut in pieces[1:]:
        level = level * one(*cut)
    return level


def centred(stream_key, dims, scale, limit, cuts=(), kind=jnp.bfloat16):
    factor_of = shard_levels(stream_key, dims, cuts, -0.22, 0.18) if cuts else 1.0
    values = jax.random.normal(stream_key, dims, jnp.float32) * scale * factor_of
    return jnp.minimum(jnp.maximum(values, -limit), limit).astype(kind)


def setup_inputs(seed: int = 0) -> dict:
    keys = jax.random.split(jax.random.key(seed), 6)
    return {
        "density": centred(keys[0], (NZ, NY, NX), 1.0, 6.0, ((0, 128), (1, 2), (2, 2)), jnp.float32),
        "bins": draw_bins(jax.random.fold_in(keys[5], 71), 0),
        "tf_color": jnp.clip(jax.random.uniform(keys[2], (3, TFBINS), jnp.float32, 0.5, 4.0), 0.5, 4.0).astype(jnp.bfloat16),
        "tf_opacity": jnp.clip(jnp.exp(jax.random.uniform(keys[3], (1, TFBINS), jnp.float32, math.log(0.0009994507), math.log(0.039794922))), 0.0009994507, 0.039794922).astype(jnp.bfloat16),
        "view_back": touch_ends(jax.random.randint(keys[4], (NX,), 0, 2), jax.random.fold_in(keys[4], 1), 0, 1).astype(jnp.int32),
    }


AMBIENT = 0.2
DIFFUSE = 1.6
LIGHT_X = 0.36
LIGHT_Y = 0.48
LIGHT_Z = 0.8

def composite(padded, bins, table, reverse):

    def visit(accum, step):
        if reverse:
            layer = (NZ - 1 - step).astype(jnp.int32)
        else:
            layer = step.astype(jnp.int32)
        slab = lax.dynamic_slice_in_dim(padded, layer, 3, 0)
        grad_z = (slab[2, 1:-1, 1:-1] - slab[0, 1:-1, 1:-1]) * 0.5
        grad_y = (slab[1, 2:, 1:-1] - slab[1, :-2, 1:-1]) * 0.5
        grad_x = (slab[1, 1:-1, 2:] - slab[1, 1:-1, :-2]) * 0.5
        shade = AMBIENT + DIFFUSE * jnp.abs(grad_x * LIGHT_X + grad_y * LIGHT_Y + grad_z * LIGHT_Z) / jnp.sqrt(1.0 + grad_x * grad_x + grad_y * grad_y + grad_z * grad_z)
        layer_bins = lax.dynamic_index_in_dim(bins, layer, 0, keepdims=False)
        looked = table[:, layer_bins]
        alpha = looked[3]
        voxel = jnp.concatenate([alpha[None] * shade[None] * looked[0:3], alpha[None]], axis=0)
        return (accum + (1.0 - accum[3:4]) * voxel, None)
    start = jnp.zeros((4, NY, NX), jnp.float32)
    accum, unused = lax.scan(visit, start, jnp.arange(NZ, dtype=jnp.int32))
    return accum

def reference(density, bins, tf_color, tf_opacity, view_back):
    padded = jnp.pad(density, 1)
    table = jnp.concatenate([tf_color, tf_opacity], axis=0).astype(jnp.float32)
    forward = composite(padded, bins, table, False)
    backward = composite(padded, bins, table, True)
    accum = jnp.where(view_back[None, None, :] == 1, backward, forward)
    return accum.reshape(4, N_GY, N_GZ, FR, NX)
```

```python
import jax
import jax.numpy as jnp
from jax import lax
from jax.experimental import pallas as pl
from jax.experimental.pallas import tpu as pltpu
from jax.sharding import PartitionSpec as P

AMBIENT = 0.2
DIFFUSE = 1.6
LIGHT_X = 0.36
LIGHT_Y = 0.48
LIGHT_Z = 0.8

MESH = pl.DeviceIdType.MESH
NZC = 8
NYC = 8
STEPS = 4


def over(front, front_alpha, back):
    return front + (1.0 - front_alpha) * back


def pair(lower, upper, flip):
    w_lower = jnp.where(flip, 1.0 - upper[3], 1.0)
    w_upper = jnp.where(flip, 1.0, 1.0 - lower[3])
    out = [w_lower * lower[c] + w_upper * upper[c] for c in range(3)]
    out.append(lower[3] + (1.0 - lower[3]) * upper[3])
    return out


def kernel(
    density, bins, color, opacity, view, out,
    dens, bin_v, coef, zh, xh, xsend, xrecv, part, drecv, ysend, yrecv, zsend, zrecv,
    in_sem, zh_s, zh_r, x_s, x_r, yh_s, yh_r, d_s, d_r, y_s, y_r, z_s, z_r,
):
    g = lax.axis_index("gz")
    gy = lax.axis_index("gy")
    gx = lax.axis_index("gx")
    z = lax.div(g, 16)
    y = lax.rem(lax.div(g, 2), 8)
    k = lax.rem(g, 2)
    g_prev = lax.rem(g + 127, 128)
    g_next = lax.rem(g + 1, 128)
    sibling = g + 1 - 2 * k

    def at(zz, yy, kk):
        return ((zz * 8 + yy) * 2 + kk, gy, gx)

    barrier = pltpu.get_barrier_semaphore()

    def greet(target):
        pl.semaphore_signal(barrier, inc=1, device_id=target, device_id_type=MESH)

    greet((g_prev, gy, gx))
    greet((g_next, gy, gx))
    greet((g, gy, 1 - gx))
    greet((g, 1 - gy, gx))
    for j in range(1, 8):
        greet(at(z, lax.rem(y + j, 8), k))
        greet(at(lax.rem(z + j, 8), y, 0))
        greet(at(lax.rem(z + j, 8), y, 1))

    load_d = pltpu.make_async_copy(density, dens.at[:, pl.ds(8, 256), :], in_sem.at[0])
    load_b = pltpu.make_async_copy(bins, bin_v, in_sem.at[1])
    load_d.start()
    load_b.start()

    zero_row = pl.multiple_of(gy * 264, 8)
    dens[:, pl.ds(zero_row, 8), :] = jnp.zeros((2, 8, 256), jnp.float32)

    lane = lax.broadcasted_iota(jnp.int32, (8, 128), 1)
    sub = lax.broadcasted_iota(jnp.int32, (8, 128), 0)

    view_rows = view[...].reshape(1, 256)
    flips = [jnp.broadcast_to(view_rows[:, 128 * h:128 * h + 128], (8, 128)) == 1 for h in range(2)]

    load_d.wait()
    edge = pl.multiple_of((1 - gx) * 128, 128)
    packed = jnp.zeros((8, 128), jnp.float32)
    for layer in range(2):
        for t in range(32):
            i = layer * 32 + t
            tile = dens[layer, pl.ds(8 + 8 * t, 8), pl.ds(edge, 128)]
            tile = jnp.where(gx == 0, pltpu.roll(tile, i + 1, 1), pltpu.roll(tile, i, 1))
            packed = jnp.where(lane == i, tile, packed)
    xsend[...] = packed

    def owner_a(zz, s):
        return lax.rem(zz + 4 + s, 8)

    def owner_b(zz, s):
        return lax.rem(zz + 11 - s, 8)

    load_b.wait()
    tables = jnp.concatenate([color[...].astype(jnp.float32), opacity[...].astype(jnp.float32)], axis=0)
    table = [[jnp.broadcast_to(tables[c:c + 1, 128 * h:128 * h + 128], (8, 128)) for h in range(2)] for c in range(4)]

    def look(entry):
        low = jnp.bitwise_and(entry, 127)
        high = entry >= 128
        return [
            jnp.where(
                high,
                jnp.take_along_axis(table[c][1], low, axis=1, mode="promise_in_bounds"),
                jnp.take_along_axis(table[c][0], low, axis=1, mode="promise_in_bounds"),
            )
            for c in range(4)
        ]

    def lookup_block(j, carry):
        s = lax.div(j, 2)
        ab = lax.rem(j, 2)
        zb = jnp.where(ab == 0, owner_a(z, s), owner_b(z, s))
        for m in range(4):
            row = pl.multiple_of(32 * zb + 8 * m, 8)
            for h in range(2):
                cols = pl.ds(128 * h, 128)
                near = look(bin_v[0, pl.ds(row, 8), cols])
                far = look(bin_v[1, pl.ds(row, 8), cols])
                k_near = jnp.where(flips[h], 1.0 - far[3], 1.0) * near[3]
                k_far = jnp.where(flips[h], 1.0, 1.0 - near[3]) * far[3]
                for c in range(3):
                    coef[c, pl.ds(row, 8), cols] = k_near * near[c]
                    coef[3 + c, pl.ds(row, 8), cols] = k_far * far[c]
                part[s, h, 3, ab, pl.ds(8 * m, 8), :] = near[3] + (1.0 - near[3]) * far[3]
        return carry

    lax.fori_loop(0, 8, lookup_block, 0)

    pl.semaphore_wait(barrier, 25)

    x_copy = pltpu.make_async_remote_copy(
        src_ref=xsend, dst_ref=xrecv, send_sem=x_s, recv_sem=x_r,
        device_id=(g, gy, 1 - gx), device_id_type=MESH)
    x_copy.start()
    y_from = pl.multiple_of(jnp.where(gy == 0, 256, 8), 8)
    y_to = pl.multiple_of(jnp.where(gy == 0, 0, 264), 8)
    yh_copy = pltpu.make_async_remote_copy(
        src_ref=dens.at[:, pl.ds(y_from, 8), :], dst_ref=dens.at[:, pl.ds(y_to, 8), :],
        send_sem=yh_s, recv_sem=yh_r, device_id=(g, 1 - gy, gx), device_id_type=MESH)
    yh_copy.start()

    def z_copy(up, j):
        target = g_next if up else g_prev
        tz = lax.div(target, 16)
        s = lax.div(j, 2)
        zb = jnp.where(lax.rem(j, 2) == 0, owner_a(tz, s), owner_b(tz, s))
        row = pl.multiple_of(32 * zb, 32)
        slot = 0 if up else 1
        return pltpu.make_async_remote_copy(
            src_ref=dens.at[1 if up else 0, pl.ds(8 + row, 32), :],
            dst_ref=zh.at[slot, pl.ds(row, 32), :],
            send_sem=zh_s.at[slot, j], recv_sem=zh_r.at[slot, j],
            device_id=(target, gy, gx), device_id_type=MESH)

    def z_start(j, carry):
        z_copy(True, j).start()
        z_copy(False, j).start()
        return carry

    lax.fori_loop(0, 8, z_start, 0)

    x_copy.wait_recv()
    columns = xrecv[...]
    for layer in range(2):
        for t in range(32):
            i = layer * 32 + t
            xh[layer, pl.ds(8 * t, 8), :] = jnp.broadcast_to(columns[:, i:i + 1], (8, 128))
    yh_copy.wait_recv()

    def shade_block(j, carry):
        s = lax.div(j, 2)
        ab = lax.rem(j, 2)
        zb = jnp.where(ab == 0, owner_a(z, s), owner_b(z, s))
        base = pl.multiple_of(32 * zb, 32)
        for slot in range(2):
            pltpu.make_async_copy(
                zh.at[slot, pl.ds(base, 32), :], zh.at[slot, pl.ds(base, 32), :], zh_r.at[slot, j]).wait()
        first = g == 0
        last = g == 127
        tiles = [[[dens[layer, pl.ds(pl.multiple_of(base + 8 * t, 8), 8), pl.ds(128 * h, 128)] for h in range(2)]
                  for t in range(6)] for layer in range(2)]
        for m in range(4):
            row = pl.multiple_of(base + 8 * m, 8)
            shades = []
            for layer in range(2):
                before, here, after = tiles[layer][m], tiles[layer][m + 1], tiles[layer][m + 2]
                side = xh[layer, pl.ds(row, 8), :]
                ends = [jnp.where(gx == 1, side, 0.0), jnp.where(gx == 0, side, 0.0)]
                to_right = [pltpu.roll(here[h], 1, 1) for h in range(2)]
                to_left = [pltpu.roll(here[h], 127, 1) for h in range(2)]
                left = [jnp.where(lane == 0, ends[0], to_right[0]), jnp.where(lane == 0, to_right[0], to_right[1])]
                right = [jnp.where(lane == 127, to_left[1], to_left[0]), jnp.where(lane == 127, ends[1], to_left[1])]
                for h in range(2):
                    cols = pl.ds(128 * h, 128)
                    above = jnp.where(sub == 0, pltpu.roll(before[h], 1, 0), pltpu.roll(here[h], 1, 0))
                    below = jnp.where(sub == 7, pltpu.roll(after[h], 7, 0), pltpu.roll(here[h], 7, 0))
                    other = tiles[1 - layer][m + 1][h]
                    if layer == 0:
                        dz = other - jnp.where(first, 0.0, zh[0, pl.ds(row, 8), cols])
                    else:
                        dz = jnp.where(last, 0.0, zh[1, pl.ds(row, 8), cols]) - other
                    dx = right[h] - left[h]
                    dy = below - above
                    dot = dx * (0.5 * DIFFUSE * LIGHT_X) + dy * (0.5 * DIFFUSE * LIGHT_Y) + dz * (0.5 * DIFFUSE * LIGHT_Z)
                    norm = 1.0 + 0.25 * (dx * dx + dy * dy + dz * dz)
                    shades.append(AMBIENT + jnp.abs(dot) * lax.rsqrt(norm))
            for h in range(2):
                cols = pl.ds(128 * h, 128)
                for c in range(3):
                    part[s, h, c, ab, pl.ds(8 * m, 8), :] = (
                        coef[c, pl.ds(row, 8), cols] * shades[h] + coef[3 + c, pl.ds(row, 8), cols] * shades[2 + h])
        return carry

    def d_copy(s):
        return pltpu.make_async_remote_copy(
            src_ref=part.at[s, 1 - k], dst_ref=drecv.at[s], send_sem=d_s.at[s], recv_sem=d_r.at[s],
            device_id=(sibling, gy, gx), device_id_type=MESH)

    flip = jnp.where(k == 0, flips[0].astype(jnp.int32), flips[1].astype(jnp.int32)) == 1
    own_front = jnp.where(flip, 1, 0) == k

    def y_copy(s, j):
        yy = lax.rem(y + j, 8)
        return pltpu.make_async_remote_copy(
            src_ref=ysend.at[s, yy], dst_ref=yrecv.at[s, y], send_sem=y_s.at[s], recv_sem=y_r.at[s],
            device_id=at(z, yy, k), device_id_type=MESH)

    def merge_pack(s):
        d_copy(s).wait_recv()
        for m in range(4):
            rows = pl.ds(8 * m, 8)
            merged = []
            for ab in range(2):
                own = [part[s, k, c, ab, rows, :] for c in range(4)]
                sib = [drecv[s, c, ab, rows, :] for c in range(4)]
                front = [jnp.where(own_front, own[c], sib[c]) for c in range(4)]
                back = [jnp.where(own_front, sib[c], own[c]) for c in range(4)]
                merged.append([over(front[c], front[3], back[c]) for c in range(4)])
            for c in range(4):
                a, b = merged[0][c], merged[1][c]
                ysend[s, 2 * m, c] = jnp.where(sub < 4, a, pltpu.roll(b, 4, 0))
                ysend[s, 2 * m + 1, c] = jnp.where(sub < 4, pltpu.roll(a, 4, 0), b)
        yrecv[s, y] = ysend[s, y]
        for j in (4, 3, 5, 2, 6, 1, 7):
            y_copy(s, j).start()

    def step(s, carry):
        lax.fori_loop(2 * s, 2 * s + 2, shade_block, 0)
        d_copy(s).start()

        @pl.when(s >= 1)
        def _():
            merge_pack(s - 1)
        return carry

    lax.fori_loop(0, STEPS, step, 0)
    merge_pack(STEPS - 1)

    def z_target(s, ab):
        return owner_a(z, s) if ab == 0 else owner_b(z, s)

    def z_send(s, carry):
        pltpu.make_async_copy(yrecv.at[s, pl.ds(0, 7)], yrecv.at[s, pl.ds(0, 7)], y_r.at[s]).wait()
        level = [[yrecv[s, i, c] for c in range(4)] for i in range(8)]
        while len(level) > 1:
            level = [pair(level[i], level[i + 1], flip) for i in range(0, len(level), 2)]
        total = level[0]
        for ab in range(2):
            for kk in range(2):
                d = 2 * ab + kk
                piece = pltpu.roll(total[0], (8 - 2 * d) % 8, 0) if d else total[0]
                for c in range(1, 4):
                    shift = (2 * c - 2 * d) % 8
                    moved = pltpu.roll(total[c], shift, 0) if shift else total[c]
                    piece = jnp.where(sub < 2 * c, piece, moved)
                zsend[s, ab, kk] = piece
                zt = z_target(s, ab)
                mine = jnp.logical_and(zt == z, k == kk)

                @pl.when(mine)
                def _():
                    zrecv[2 * z + k] = piece

                @pl.when(jnp.logical_not(mine))
                def _():
                    pltpu.make_async_remote_copy(
                        src_ref=zsend.at[s, ab, kk], dst_ref=zrecv.at[2 * z + k], send_sem=z_s, recv_sem=z_r,
                        device_id=at(zt, y, kk), device_id_type=MESH).start()
        return carry

    lax.fori_loop(0, STEPS, z_send, 0)

    pltpu.make_async_copy(zrecv.at[pl.ds(0, 15)], zrecv.at[pl.ds(0, 15)], z_r).wait()
    for h in range(2):
        level = []
        for i in range(8):
            value = zrecv[2 * i + h]
            spread = jnp.where(sub >= 6, value, pltpu.roll(value, 6, 0))
            spread = jnp.where(sub >= 4, spread, pltpu.roll(spread, 4, 0))
            level.append((value, spread))
        while len(level) > 1:
            merged = []
            for i in range(0, len(level), 2):
                (lv, la), (uv, ua) = level[i], level[i + 1]
                fv, fa = jnp.where(flips[h], uv, lv), jnp.where(flips[h], ua, la)
                bv, ba = jnp.where(flips[h], lv, uv), jnp.where(flips[h], la, ua)
                merged.append((over(fv, fa, bv), over(fa, fa, ba)))
            level = merged
        for c in range(4):
            out[c, :, pl.ds(128 * h, 128)] = level[0][0][2 * c:2 * c + 2, :]

    x_copy.wait_send()
    yh_copy.wait_send()

    def z_drain(j, carry):
        z_copy(True, j).wait_send()
        z_copy(False, j).wait_send()
        return carry

    lax.fori_loop(0, 8, z_drain, 0)

    def s_drain(s, carry):
        d_copy(s).wait_send()
        pltpu.make_async_copy(ysend.at[s, pl.ds(0, 7)], ysend.at[s, pl.ds(0, 7)], y_s.at[s]).wait()
        return carry

    lax.fori_loop(0, STEPS, s_drain, 0)
    pltpu.make_async_copy(zrecv.at[pl.ds(0, 15)], zrecv.at[pl.ds(0, 15)], z_s).wait()


def local(density, bins, tf_color, tf_opacity, view_back):
    f32 = jnp.float32
    vmem = pl.BlockSpec(memory_space=pltpu.VMEM)
    anyspace = pl.BlockSpec(memory_space=pl.ANY)
    dma = pltpu.SemaphoreType.DMA
    result = pl.pallas_call(
        kernel,
        out_shape=jax.ShapeDtypeStruct((4, 2, 256), f32),
        in_specs=[anyspace, anyspace, vmem, vmem, vmem],
        out_specs=vmem,
        scratch_shapes=[
            pltpu.VMEM((2, 272, 256), f32),
            pltpu.VMEM((2, 256, 256), jnp.int32),
            pltpu.VMEM((6, 256, 256), f32),
            pltpu.VMEM((2, 256, 256), f32),
            pltpu.VMEM((2, 256, 128), f32),
            pltpu.VMEM((8, 128), f32),
            pltpu.VMEM((8, 128), f32),
            pltpu.VMEM((STEPS, 2, 4, 2, 32, 128), f32),
            pltpu.VMEM((STEPS, 4, 2, 32, 128), f32),
            pltpu.VMEM((STEPS, 8, 4, 8, 128), f32),
            pltpu.VMEM((STEPS, 8, 4, 8, 128), f32),
            pltpu.VMEM((STEPS, 2, 2, 8, 128), f32),
            pltpu.VMEM((16, 8, 128), f32),
            dma((2,)),
            dma((2, 8)),
            dma((2, 8)),
            dma, dma, dma, dma,
            dma((STEPS,)),
            dma((STEPS,)),
            dma((STEPS,)),
            dma((STEPS,)),
            dma, dma,
        ],
        compiler_params=pltpu.CompilerParams(
            collective_id=0, has_side_effects=True, vmem_limit_bytes=32 << 20),
    )(density, bins, tf_color, tf_opacity, view_back)
    return result.reshape(4, 1, 1, 2, 256)


def solution(mesh):
    return jax.shard_map(
        local,
        mesh=mesh,
        in_specs=(P("gz", "gy", "gx"), P("gz", "gy", "gx"), P(), P(), P("gx")),
        out_specs=P(None, "gy", "gz", None, "gx"),
        check_vma=False,
    )
```

```python
import jax
import jax.numpy as jnp
from jax import lax
from jax.experimental import pallas as pl
from jax.experimental.pallas import tpu as pltpu
from jax.sharding import PartitionSpec as P

AMBIENT = 0.2
DIFFUSE = 1.6
LIGHT_X = 0.36
LIGHT_Y = 0.48
LIGHT_Z = 0.8

MESH = pl.DeviceIdType.MESH
STEPS = 8
LAG = 4
Y_ORDER = (0, 1, 7, 2, 6, 3, 5, 4)


def over(front, front_alpha, back):
    return front + (1.0 - front_alpha) * back


def kernel(
    density, bins, color_h, opacity_h, view_h, out,
    color, opacity, view, dens, bin_v, coef, zh, xh, xsend, xrecv, part, drecv, ysend, yrecv, zsend, zrecv,
    in_sem, zh_s, zh_r, x_s, x_r, yh_s, yh_r, d_s, d_r, y_s, y_r, z_s, z_r, y_ready, z_ready,
):
    g = lax.axis_index("gz")
    gy = lax.axis_index("gy")
    gx = lax.axis_index("gx")
    z = lax.div(g, 16)
    y = lax.rem(lax.div(g, 2), 8)
    k = lax.rem(g, 2)
    g_prev = lax.rem(g + 127, 128)
    g_next = lax.rem(g + 1, 128)
    sibling = g + 1 - 2 * k

    def at(zz, yy, kk):
        return ((zz * 8 + yy) * 2 + kk, gy, gx)

    barrier = pltpu.get_barrier_semaphore()

    def greet(target):
        pl.semaphore_signal(barrier, inc=1, device_id=target, device_id_type=MESH)

    greet((g, 1 - gy, gx))
    greet((g_prev, gy, gx))
    greet((g_next, gy, gx))
    greet((g, gy, 1 - gx))
    for j in (1, 7, 2, 6):
        greet(at(z, lax.rem(y + j, 8), k))
        greet(at(lax.rem(z + j, 8), y, 0))
        greet(at(lax.rem(z + j, 8), y, 1))

    load_d = pltpu.make_async_copy(density, dens.at[:, pl.ds(8, 256), :], in_sem.at[0])
    load_b = pltpu.make_async_copy(bins, bin_v, in_sem.at[1])
    load_d.start()
    load_b.start()
    loads = [
        pltpu.make_async_copy(src, dst, in_sem.at[2 + i])
        for i, (src, dst) in enumerate(((color_h, color), (opacity_h, opacity), (view_h, view)))
    ]
    for copy in loads:
        copy.start()

    zero_row = pl.multiple_of(gy * 264, 8)
    dens[:, pl.ds(zero_row, 8), :] = jnp.zeros((2, 8, 256), jnp.float32)

    lane = lax.broadcasted_iota(jnp.int32, (8, 128), 1)
    sub = lax.broadcasted_iota(jnp.int32, (8, 128), 0)

    for copy in loads:
        copy.wait()
    view_rows = view[...].reshape(1, 256)
    flips = [jnp.broadcast_to(view_rows[:, 128 * h:128 * h + 128], (8, 128)) == 1 for h in range(2)]

    load_d.wait()
    edge = pl.multiple_of((1 - gx) * 128, 128)
    packed = jnp.zeros((8, 128), jnp.float32)
    for layer in range(2):
        for t in range(32):
            i = layer * 32 + t
            tile = dens[layer, pl.ds(8 + 8 * t, 8), pl.ds(edge, 128)]
            tile = jnp.where(gx == 0, pltpu.roll(tile, i + 1, 1), pltpu.roll(tile, i, 1))
            packed = jnp.where(lane == i, tile, packed)
    xsend[...] = packed

    load_b.wait()
    tables = jnp.concatenate([color[...].astype(jnp.float32), opacity[...].astype(jnp.float32)], axis=0)
    table = [[jnp.broadcast_to(tables[c:c + 1, 128 * h:128 * h + 128], (8, 128)) for h in range(2)] for c in range(4)]

    def look(entry):
        low = jnp.bitwise_and(entry, 127)
        high = entry >= 128
        return [
            jnp.where(
                high,
                jnp.take_along_axis(table[c][1], low, axis=1, mode="promise_in_bounds"),
                jnp.take_along_axis(table[c][0], low, axis=1, mode="promise_in_bounds"),
            )
            for c in range(4)
        ]

    def lookup_block(s, carry):
        for m in range(4):
            row = pl.multiple_of(32 * s + 8 * m, 8)
            for h in range(2):
                cols = pl.ds(128 * h, 128)
                near = look(bin_v[0, pl.ds(row, 8), cols])
                far = look(bin_v[1, pl.ds(row, 8), cols])
                k_near = jnp.where(flips[h], 1.0 - far[3], 1.0) * near[3]
                k_far = jnp.where(flips[h], 1.0, 1.0 - near[3]) * far[3]
                for c in range(3):
                    coef[c, pl.ds(row, 8), cols] = k_near * near[c]
                    coef[3 + c, pl.ds(row, 8), cols] = k_far * far[c]
                part[s, h, 3, pl.ds(8 * m, 8), :] = near[3] + (1.0 - near[3]) * far[3]
        return carry

    lax.fori_loop(0, 8, lookup_block, 0)

    pl.semaphore_wait(barrier, 16)

    x_copy = pltpu.make_async_remote_copy(
        src_ref=xsend, dst_ref=xrecv, send_sem=x_s, recv_sem=x_r,
        device_id=(g, gy, 1 - gx), device_id_type=MESH)
    x_copy.start()
    y_from = pl.multiple_of(jnp.where(gy == 0, 256, 8), 8)
    y_to = pl.multiple_of(jnp.where(gy == 0, 0, 264), 8)
    yh_copy = pltpu.make_async_remote_copy(
        src_ref=dens.at[:, pl.ds(y_from, 8), :], dst_ref=dens.at[:, pl.ds(y_to, 8), :],
        send_sem=yh_s, recv_sem=yh_r, device_id=(g, 1 - gy, gx), device_id_type=MESH)
    yh_copy.start()

    def z_copy(up, j):
        target = g_next if up else g_prev
        row = pl.multiple_of(32 * j, 32)
        slot = 0 if up else 1
        return pltpu.make_async_remote_copy(
            src_ref=dens.at[1 if up else 0, pl.ds(8 + row, 32), :],
            dst_ref=zh.at[slot, pl.ds(row, 32), :],
            send_sem=zh_s.at[slot, j], recv_sem=zh_r.at[slot, j],
            device_id=(target, gy, gx), device_id_type=MESH)

    def z_start(j, carry):
        z_copy(True, j).start()
        z_copy(False, j).start()
        return carry

    lax.fori_loop(0, 8, z_start, 0)

    for j in (2, 6):
        pl.semaphore_signal(y_ready, inc=1, device_id=at(z, lax.rem(y + j, 8), k), device_id_type=MESH)
    for j in (2, 6):
        for kk in range(2):
            pl.semaphore_signal(z_ready, inc=1, device_id=at(lax.rem(z + j, 8), y, kk), device_id_type=MESH)

    x_copy.wait_recv()
    columns = xrecv[...]
    for layer in range(2):
        for t in range(32):
            i = layer * 32 + t
            xh[layer, pl.ds(8 * t, 8), :] = jnp.broadcast_to(columns[:, i:i + 1], (8, 128))
    yh_copy.wait_recv()

    def shade_block(s):
        base = pl.multiple_of(32 * s, 32)
        for slot in range(2):
            pltpu.make_async_copy(
                zh.at[slot, pl.ds(base, 32), :], zh.at[slot, pl.ds(base, 32), :], zh_r.at[slot, s]).wait()
        first = g == 0
        last = g == 127
        tiles = [[[dens[layer, pl.ds(pl.multiple_of(base + 8 * t, 8), 8), pl.ds(128 * h, 128)] for h in range(2)]
                  for t in range(6)] for layer in range(2)]
        for m in range(4):
            row = pl.multiple_of(base + 8 * m, 8)
            shades = []
            for layer in range(2):
                before, here, after = tiles[layer][m], tiles[layer][m + 1], tiles[layer][m + 2]
                side = xh[layer, pl.ds(row, 8), :]
                ends = [jnp.where(gx == 1, side, 0.0), jnp.where(gx == 0, side, 0.0)]
                to_right = [pltpu.roll(here[h], 1, 1) for h in range(2)]
                to_left = [pltpu.roll(here[h], 127, 1) for h in range(2)]
                left = [jnp.where(lane == 0, ends[0], to_right[0]), jnp.where(lane == 0, to_right[0], to_right[1])]
                right = [jnp.where(lane == 127, to_left[1], to_left[0]), jnp.where(lane == 127, ends[1], to_left[1])]
                for h in range(2):
                    cols = pl.ds(128 * h, 128)
                    above = jnp.where(sub == 0, pltpu.roll(before[h], 1, 0), pltpu.roll(here[h], 1, 0))
                    below = jnp.where(sub == 7, pltpu.roll(after[h], 7, 0), pltpu.roll(here[h], 7, 0))
                    other = tiles[1 - layer][m + 1][h]
                    if layer == 0:
                        dz = other - jnp.where(first, 0.0, zh[0, pl.ds(row, 8), cols])
                    else:
                        dz = jnp.where(last, 0.0, zh[1, pl.ds(row, 8), cols]) - other
                    dx = right[h] - left[h]
                    dy = below - above
                    dot = dx * (0.5 * DIFFUSE * LIGHT_X) + dy * (0.5 * DIFFUSE * LIGHT_Y) + dz * (0.5 * DIFFUSE * LIGHT_Z)
                    norm = 1.0 + 0.25 * (dx * dx + dy * dy + dz * dz)
                    shades.append(AMBIENT + jnp.abs(dot) * lax.rsqrt(norm))
            for h in range(2):
                cols = pl.ds(128 * h, 128)
                for c in range(3):
                    part[s, h, c, pl.ds(8 * m, 8), :] = (
                        coef[c, pl.ds(row, 8), cols] * shades[h] + coef[3 + c, pl.ds(row, 8), cols] * shades[2 + h])

    def d_copy(s):
        return pltpu.make_async_remote_copy(
            src_ref=part.at[s, 1 - k], dst_ref=drecv.at[s], send_sem=d_s.at[s], recv_sem=d_r.at[s],
            device_id=(sibling, gy, gx), device_id_type=MESH)

    flip = jnp.where(k == 0, flips[0].astype(jnp.int32), flips[1].astype(jnp.int32)) == 1
    own_front = jnp.where(flip, 1, 0) == k

    def y_copy(s, yy):
        return pltpu.make_async_remote_copy(
            src_ref=ysend.at[s, yy], dst_ref=yrecv.at[s, y], send_sem=y_s.at[s], recv_sem=y_r.at[s],
            device_id=at(z, yy, k), device_id_type=MESH)

    def merge_pack(s):
        d_copy(s).wait_recv()
        for m in range(4):
            rows = pl.ds(8 * m, 8)
            own = [part[s, k, c, rows, :] for c in range(4)]
            sib = [drecv[s, c, rows, :] for c in range(4)]
            front = [jnp.where(own_front, own[c], sib[c]) for c in range(4)]
            back = [jnp.where(own_front, sib[c], own[c]) for c in range(4)]
            merged = [over(front[c], front[3], back[c]) for c in range(4)]
            turned = [pltpu.roll(merged[c], 4, 0) for c in range(4)]
            for c in range(2):
                ysend[s, 2 * m, c] = jnp.where(sub < 4, merged[2 * c], turned[2 * c + 1])
                ysend[s, 2 * m + 1, c] = jnp.where(sub < 4, turned[2 * c], merged[2 * c + 1])
        yrecv[s, y] = ysend[s, y]
        for yy in Y_ORDER:
            @pl.when(yy != y)
            def _():
                y_copy(s, yy).start()

    def z_send(s):
        pltpu.make_async_copy(yrecv.at[s, pl.ds(0, 7)], yrecv.at[s, pl.ds(0, 7)], y_r.at[s]).wait()
        level = []
        for i in range(8):
            rg, ba = yrecv[s, i, 0], yrecv[s, i, 1]
            level.append((rg, ba, jnp.where(sub < 4, pltpu.roll(ba, 4, 0), ba)))
        while len(level) > 1:
            merged = []
            for i in range(0, len(level), 2):
                lower, upper = level[i], level[i + 1]
                w_lower = jnp.where(flip, 1.0 - upper[2], 1.0)
                w_upper = jnp.where(flip, 1.0, 1.0 - lower[2])
                merged.append(tuple(w_lower * a + w_upper * b for a, b in zip(lower, upper)))
            level = merged
        rg, ba, _ = level[0]
        for kk in range(2):
            piece = None
            for c, (value, at_row) in enumerate(((rg, 0), (rg, 4), (ba, 0), (ba, 4))):
                shift = (2 * c - at_row - 2 * kk) % 8
                moved = pltpu.roll(value, shift, 0) if shift else value
                piece = moved if piece is None else jnp.where(sub < 2 * c, piece, moved)
            zsend[2 * s + kk] = piece
            mine = jnp.logical_and(s == z, k == kk)

            @pl.when(mine)
            def _():
                zrecv[2 * z + k] = piece

            @pl.when(jnp.logical_not(mine))
            def _():
                pltpu.make_async_remote_copy(
                    src_ref=zsend.at[2 * s + kk], dst_ref=zrecv.at[2 * z + k], send_sem=z_s, recv_sem=z_r,
                    device_id=at(s, y, kk), device_id_type=MESH).start()

    def step(s, carry):
        @pl.when(s < STEPS)
        def _():
            shade_block(s)
            d_copy(s).start()

        @pl.when(s == 1)
        def _():
            pl.semaphore_wait(y_ready, 2)

        @pl.when(jnp.logical_and(s >= 1, s < STEPS + 1))
        def _():
            merge_pack(s - 1)

        @pl.when(s == LAG)
        def _():
            pl.semaphore_wait(z_ready, 4)

        @pl.when(s >= LAG)
        def _():
            z_send(s - LAG)
        return carry

    lax.fori_loop(0, STEPS + LAG, step, 0)

    pltpu.make_async_copy(zrecv.at[pl.ds(0, 15)], zrecv.at[pl.ds(0, 15)], z_r).wait()
    for h in range(2):
        level = []
        for i in range(8):
            value = zrecv[2 * i + h]
            spread = jnp.where(sub >= 6, value, pltpu.roll(value, 6, 0))
            spread = jnp.where(sub >= 4, spread, pltpu.roll(spread, 4, 0))
            level.append((value, spread))
        while len(level) > 1:
            merged = []
            for i in range(0, len(level), 2):
                (lv, la), (uv, ua) = level[i], level[i + 1]
                fv, fa = jnp.where(flips[h], uv, lv), jnp.where(flips[h], ua, la)
                bv, ba = jnp.where(flips[h], lv, uv), jnp.where(flips[h], la, ua)
                merged.append((over(fv, fa, bv), over(fa, fa, ba)))
            level = merged
        for c in range(4):
            out[c, :, pl.ds(128 * h, 128)] = level[0][0][2 * c:2 * c + 2, :]

    x_copy.wait_send()
    yh_copy.wait_send()

    def z_drain(j, carry):
        z_copy(True, j).wait_send()
        z_copy(False, j).wait_send()
        return carry

    lax.fori_loop(0, 8, z_drain, 0)

    def s_drain(s, carry):
        d_copy(s).wait_send()
        pltpu.make_async_copy(ysend.at[s, pl.ds(0, 7)], ysend.at[s, pl.ds(0, 7)], y_s.at[s]).wait()
        return carry

    lax.fori_loop(0, STEPS, s_drain, 0)
    pltpu.make_async_copy(zrecv.at[pl.ds(0, 15)], zrecv.at[pl.ds(0, 15)], z_s).wait()


def local(density, bins, tf_color, tf_opacity, view_back):
    f32 = jnp.float32
    vmem = pl.BlockSpec(memory_space=pltpu.VMEM)
    hbm = pl.BlockSpec(memory_space=pltpu.HBM)
    dma = pltpu.SemaphoreType.DMA
    result = pl.pallas_call(
        kernel,
        out_shape=jax.ShapeDtypeStruct((4, 2, 256), f32),
        in_specs=[hbm] * 5,
        out_specs=vmem,
        scratch_shapes=[
            pltpu.VMEM((3, 256), jnp.bfloat16),
            pltpu.VMEM((1, 256), jnp.bfloat16),
            pltpu.VMEM((256,), jnp.int32),
            pltpu.VMEM((2, 272, 256), f32),
            pltpu.VMEM((2, 256, 256), jnp.int32),
            pltpu.VMEM((6, 256, 256), f32),
            pltpu.VMEM((2, 256, 256), f32),
            pltpu.VMEM((2, 256, 128), f32),
            pltpu.VMEM((8, 128), f32),
            pltpu.VMEM((8, 128), f32),
            pltpu.VMEM((STEPS, 2, 4, 32, 128), f32),
            pltpu.VMEM((STEPS, 4, 32, 128), f32),
            pltpu.VMEM((STEPS, 8, 2, 8, 128), f32),
            pltpu.VMEM((STEPS, 8, 2, 8, 128), f32),
            pltpu.VMEM((2 * STEPS, 8, 128), f32),
            pltpu.VMEM((16, 8, 128), f32),
            dma((5,)),
            dma((2, 8)),
            dma((2, 8)),
            dma, dma, dma, dma,
            dma((STEPS,)),
            dma((STEPS,)),
            dma((STEPS,)),
            dma((STEPS,)),
            dma, dma,
            pltpu.SemaphoreType.REGULAR,
            pltpu.SemaphoreType.REGULAR,
        ],
        compiler_params=pltpu.CompilerParams(
            collective_id=0, has_side_effects=True, vmem_limit_bytes=60 << 20),
    )(density, bins, tf_color, tf_opacity, view_back)
    return result.reshape(4, 1, 1, 2, 256)


def solution(mesh):
    return jax.shard_map(
        local,
        mesh=mesh,
        in_specs=(P("gz", "gy", "gx"), P("gz", "gy", "gx"), P(), P(), P("gx")),
        out_specs=P(None, "gy", "gz", None, "gx"),
        check_vma=False,
    )
```

```python
import jax
import jax.numpy as jnp
from jax import lax
from jax.experimental import pallas as pl
from jax.experimental.pallas import tpu as pltpu
from jax.sharding import PartitionSpec as P

AMBIENT = 0.2
DIFFUSE = 1.6
LIGHT_X = 0.36
LIGHT_Y = 0.48
LIGHT_Z = 0.8

MESH = pl.DeviceIdType.MESH
STEPS = 8
LAG = 8
Y_ORDER = (0, 1, 7, 2, 6, 3, 5, 4)


def over(front, front_alpha, back):
    return front + (1.0 - front_alpha) * back


def kernel(
    density, bins, color_h, opacity_h, view_h, out,
    color, opacity, view, dens, bin_v, coef, zh, xh, xsend, xrecv, part, drecv, ysend, yrecv, zsend, zrecv,
    in_sem, zh_s, zh_r, x_s, x_r, yh_s, yh_r, d_s, d_r, y_s, y_r, z_s, z_r, y_ready, z_ready, z_all,
):
    g = lax.axis_index("gz")
    gy = lax.axis_index("gy")
    gx = lax.axis_index("gx")
    z = lax.div(g, 16)
    y = lax.rem(lax.div(g, 2), 8)
    k = lax.rem(g, 2)
    g_prev = jnp.maximum(g - 1, 0)
    g_next = jnp.minimum(g + 1, 127)
    has_prev = g > 0
    has_next = g < 127
    sibling = g + 1 - 2 * k

    def at(zz, yy, kk):
        return ((zz * 8 + yy) * 2 + kk, gy, gx)

    barrier = pltpu.get_barrier_semaphore()

    def greet(target):
        pl.semaphore_signal(barrier, inc=1, device_id=target, device_id_type=MESH)

    def if_z(j, do):
        zz = jnp.clip(z + j, 0, 7)

        @pl.when(zz == z + j)
        def _():
            do(at(zz, y, 0))
            do(at(zz, y, 1))

    def count_z(j):
        return 2 * ((z >= j).astype(jnp.int32) + (z + j <= 7).astype(jnp.int32))

    greet((g, 1 - gy, gx))
    pl.when(has_prev)(lambda: greet((g_prev, gy, gx)))
    pl.when(has_next)(lambda: greet((g_next, gy, gx)))
    greet((g, gy, 1 - gx))
    for j in (1, 2):
        greet(at(z, lax.rem(y + j, 8), k))
        greet(at(z, lax.rem(y + 8 - j, 8), k))
        if_z(j, greet)
        if_z(-j, greet)

    load_d = pltpu.make_async_copy(density, dens.at[:, pl.ds(8, 256), :], in_sem.at[0])
    load_b = pltpu.make_async_copy(bins, bin_v, in_sem.at[1])
    load_d.start()
    load_b.start()
    loads = [
        pltpu.make_async_copy(src, dst, in_sem.at[2 + i])
        for i, (src, dst) in enumerate(((color_h, color), (opacity_h, opacity), (view_h, view)))
    ]
    for copy in loads:
        copy.start()

    @pl.when(g == 0)
    def _():
        zh[0] = jnp.zeros((256, 256), jnp.float32)

    @pl.when(g == 127)
    def _():
        zh[1] = jnp.zeros((256, 256), jnp.float32)

    zero_row = pl.multiple_of(gy * 264, 8)
    dens[:, pl.ds(zero_row, 8), :] = jnp.zeros((2, 8, 256), jnp.float32)

    lane = lax.broadcasted_iota(jnp.int32, (8, 128), 1)
    sub = lax.broadcasted_iota(jnp.int32, (8, 128), 0)

    for copy in loads:
        copy.wait()
    view_rows = view[...].reshape(1, 256)
    flips = [jnp.broadcast_to(view_rows[:, 128 * h:128 * h + 128], (8, 128)) == 1 for h in range(2)]

    load_d.wait()
    edge = pl.multiple_of((1 - gx) * 128, 128)
    packed = jnp.zeros((8, 128), jnp.float32)
    for layer in range(2):
        for t in range(32):
            i = layer * 32 + t
            tile = dens[layer, pl.ds(8 + 8 * t, 8), pl.ds(edge, 128)]
            tile = jnp.where(gx == 0, pltpu.roll(tile, i + 1, 1), pltpu.roll(tile, i, 1))
            packed = jnp.where(lane == i, tile, packed)
    xsend[...] = packed

    load_b.wait()
    tables = jnp.concatenate([color[...].astype(jnp.float32), opacity[...].astype(jnp.float32)], axis=0)
    table = [[jnp.broadcast_to(tables[c:c + 1, 128 * h:128 * h + 128], (8, 128)) for h in range(2)] for c in range(4)]

    def look(entry):
        low = jnp.bitwise_and(entry, 127)
        high = entry >= 128
        return [
            jnp.where(
                high,
                jnp.take_along_axis(table[c][1], low, axis=1, mode="promise_in_bounds"),
                jnp.take_along_axis(table[c][0], low, axis=1, mode="promise_in_bounds"),
            )
            for c in range(4)
        ]

    def lookup_block(s, carry):
        for m in range(4):
            row = pl.multiple_of(32 * s + 8 * m, 8)
            for h in range(2):
                cols = pl.ds(128 * h, 128)
                near = look(bin_v[0, pl.ds(row, 8), cols])
                far = look(bin_v[1, pl.ds(row, 8), cols])
                k_near = jnp.where(flips[h], 1.0 - far[3], 1.0) * near[3]
                k_far = jnp.where(flips[h], 1.0, 1.0 - near[3]) * far[3]
                for c in range(3):
                    coef[c, pl.ds(row, 8), cols] = k_near * near[c]
                    coef[3 + c, pl.ds(row, 8), cols] = k_far * far[c]
                part[s, h, 3, pl.ds(8 * m, 8), :] = near[3] + (1.0 - near[3]) * far[3]
        return carry

    lax.fori_loop(0, 8, lookup_block, 0)

    pl.semaphore_wait(
        barrier, 6 + has_prev.astype(jnp.int32) + has_next.astype(jnp.int32) + count_z(1) + count_z(2))

    x_copy = pltpu.make_async_remote_copy(
        src_ref=xsend, dst_ref=xrecv, send_sem=x_s, recv_sem=x_r,
        device_id=(g, gy, 1 - gx), device_id_type=MESH)
    x_copy.start()
    y_from = pl.multiple_of(jnp.where(gy == 0, 256, 8), 8)
    y_to = pl.multiple_of(jnp.where(gy == 0, 0, 264), 8)
    yh_copy = pltpu.make_async_remote_copy(
        src_ref=dens.at[:, pl.ds(y_from, 8), :], dst_ref=dens.at[:, pl.ds(y_to, 8), :],
        send_sem=yh_s, recv_sem=yh_r, device_id=(g, 1 - gy, gx), device_id_type=MESH)
    yh_copy.start()

    def z_copy(up, j):
        target = g_next if up else g_prev
        row = pl.multiple_of(32 * j, 32)
        slot = 0 if up else 1
        return pltpu.make_async_remote_copy(
            src_ref=dens.at[1 if up else 0, pl.ds(8 + row, 32), :],
            dst_ref=zh.at[slot, pl.ds(row, 32), :],
            send_sem=zh_s.at[slot, j], recv_sem=zh_r.at[slot, j],
            device_id=(target, gy, gx), device_id_type=MESH)

    def z_start(j, carry):
        @pl.when(has_next)
        def _():
            z_copy(True, j).start()

        @pl.when(has_prev)
        def _():
            z_copy(False, j).start()
        return carry

    lax.fori_loop(0, 8, z_start, 0)

    def ready(semaphore):
        return lambda target: pl.semaphore_signal(semaphore, inc=1, device_id=target, device_id_type=MESH)

    for j in (2, 6):
        ready(y_ready)(at(z, lax.rem(y + j, 8), k))
    if_z(2, ready(z_ready))
    if_z(-2, ready(z_ready))

    x_copy.wait_recv()
    columns = xrecv[...]
    for layer in range(2):
        for t in range(32):
            i = layer * 32 + t
            xh[layer, pl.ds(8 * t, 8), :] = jnp.broadcast_to(columns[:, i:i + 1], (8, 128))
    yh_copy.wait_recv()

    def shade_block(s):
        base = pl.multiple_of(32 * s, 32)
        for slot, there in ((0, has_prev), (1, has_next)):
            @pl.when(there)
            def _():
                pltpu.make_async_copy(
                    zh.at[slot, pl.ds(base, 32), :], zh.at[slot, pl.ds(base, 32), :], zh_r.at[slot, s]).wait()

        tiles = [[[dens[layer, pl.ds(pl.multiple_of(base + 8 * t, 8), 8), pl.ds(128 * h, 128)] for h in range(2)]
                  for t in range(6)] for layer in range(2)]
        for m in range(4):
            row = pl.multiple_of(base + 8 * m, 8)
            shades = []
            for layer in range(2):
                before, here, after = tiles[layer][m], tiles[layer][m + 1], tiles[layer][m + 2]
                side = xh[layer, pl.ds(row, 8), :]
                ends = [jnp.where(gx == 1, side, 0.0), jnp.where(gx == 0, side, 0.0)]
                to_right = [pltpu.roll(here[h], 1, 1) for h in range(2)]
                to_left = [pltpu.roll(here[h], 127, 1) for h in range(2)]
                left = [jnp.where(lane == 0, ends[0], to_right[0]), jnp.where(lane == 0, to_right[0], to_right[1])]
                right = [jnp.where(lane == 127, to_left[1], to_left[0]), jnp.where(lane == 127, ends[1], to_left[1])]
                for h in range(2):
                    cols = pl.ds(128 * h, 128)
                    above = jnp.where(sub == 0, pltpu.roll(before[h], 1, 0), pltpu.roll(here[h], 1, 0))
                    below = jnp.where(sub == 7, pltpu.roll(after[h], 7, 0), pltpu.roll(here[h], 7, 0))
                    other = tiles[1 - layer][m + 1][h]
                    if layer == 0:
                        dz = other - zh[0, pl.ds(row, 8), cols]
                    else:
                        dz = zh[1, pl.ds(row, 8), cols] - other
                    dx = right[h] - left[h]
                    dy = below - above
                    dot = dx * (0.5 * DIFFUSE * LIGHT_X) + dy * (0.5 * DIFFUSE * LIGHT_Y) + dz * (0.5 * DIFFUSE * LIGHT_Z)
                    norm = 1.0 + 0.25 * (dx * dx + dy * dy + dz * dz)
                    shades.append(AMBIENT + jnp.abs(dot) * lax.rsqrt(norm))
            for h in range(2):
                cols = pl.ds(128 * h, 128)
                for c in range(3):
                    part[s, h, c, pl.ds(8 * m, 8), :] = (
                        coef[c, pl.ds(row, 8), cols] * shades[h] + coef[3 + c, pl.ds(row, 8), cols] * shades[2 + h])

    def d_copy(s):
        return pltpu.make_async_remote_copy(
            src_ref=part.at[s, 1 - k], dst_ref=drecv.at[s], send_sem=d_s.at[s], recv_sem=d_r.at[s],
            device_id=(sibling, gy, gx), device_id_type=MESH)

    flip = jnp.where(k == 0, flips[0].astype(jnp.int32), flips[1].astype(jnp.int32)) == 1
    own_front = jnp.where(flip, 1, 0) == k

    def y_copy(s, yy):
        return pltpu.make_async_remote_copy(
            src_ref=ysend.at[s, yy], dst_ref=yrecv.at[s, y], send_sem=y_s.at[s], recv_sem=y_r.at[s],
            device_id=at(z, yy, k), device_id_type=MESH)

    def merge_pack(s):
        d_copy(s).wait_recv()
        for m in range(4):
            rows = pl.ds(8 * m, 8)
            own = [part[s, k, c, rows, :] for c in range(4)]
            sib = [drecv[s, c, rows, :] for c in range(4)]
            front = [jnp.where(own_front, own[c], sib[c]) for c in range(4)]
            back = [jnp.where(own_front, sib[c], own[c]) for c in range(4)]
            merged = [over(front[c], front[3], back[c]) for c in range(4)]
            turned = [pltpu.roll(merged[c], 4, 0) for c in range(4)]
            for c in range(2):
                ysend[s, 2 * m, c] = jnp.where(sub < 4, merged[2 * c], turned[2 * c + 1])
                ysend[s, 2 * m + 1, c] = jnp.where(sub < 4, turned[2 * c], merged[2 * c + 1])
        yrecv[s, y] = ysend[s, y]
        for yy in Y_ORDER:
            @pl.when(yy != y)
            def _():
                y_copy(s, yy).start()

    def z_send(s):
        pltpu.make_async_copy(yrecv.at[s, pl.ds(0, 7)], yrecv.at[s, pl.ds(0, 7)], y_r.at[s]).wait()
        level = []
        for i in range(8):
            rg, ba = yrecv[s, i, 0], yrecv[s, i, 1]
            level.append((rg, ba, jnp.where(sub < 4, pltpu.roll(ba, 4, 0), ba)))
        while len(level) > 1:
            merged = []
            for i in range(0, len(level), 2):
                lower, upper = level[i], level[i + 1]
                w_lower = jnp.where(flip, 1.0 - upper[2], 1.0)
                w_upper = jnp.where(flip, 1.0, 1.0 - lower[2])
                merged.append(tuple(w_lower * a + w_upper * b for a, b in zip(lower, upper)))
            level = merged
        rg, ba, _ = level[0]
        for kk in range(2):
            piece = None
            for c, (value, at_row) in enumerate(((rg, 0), (rg, 4), (ba, 0), (ba, 4))):
                shift = (2 * c - at_row - 2 * kk) % 8
                moved = pltpu.roll(value, shift, 0) if shift else value
                piece = moved if piece is None else jnp.where(sub < 2 * c, piece, moved)
            zsend[2 * s + kk] = piece
            mine = jnp.logical_and(s == z, k == kk)

            @pl.when(mine)
            def _():
                zrecv[2 * z + k] = piece

            @pl.when(jnp.logical_not(mine))
            def _():
                pltpu.make_async_remote_copy(
                    src_ref=zsend.at[2 * s + kk], dst_ref=zrecv.at[2 * z + k], send_sem=z_s, recv_sem=z_r,
                    device_id=at(s, y, kk), device_id_type=MESH).start()

    def step(s, carry):
        @pl.when(s < STEPS)
        def _():
            shade_block(s)
            d_copy(s).start()

        @pl.when(s == 1)
        def _():
            pl.semaphore_wait(y_ready, 2)

        @pl.when(jnp.logical_and(s >= 1, s < STEPS + 1))
        def _():
            merge_pack(s - 1)

        @pl.when(s == 3)
        def _():
            pl.semaphore_wait(z_ready, count_z(2))
            if_z(4, ready(z_all))
            if_z(-4, ready(z_all))

        @pl.when(s == LAG)
        def _():
            pl.semaphore_wait(z_all, count_z(4))

        @pl.when(s >= LAG)
        def _():
            z_send(s - LAG)
        return carry

    lax.fori_loop(0, STEPS + LAG, step, 0)

    pltpu.make_async_copy(zrecv.at[pl.ds(0, 15)], zrecv.at[pl.ds(0, 15)], z_r).wait()
    for h in range(2):
        level = []
        for i in range(8):
            value = zrecv[2 * i + h]
            spread = jnp.where(sub >= 6, value, pltpu.roll(value, 6, 0))
            spread = jnp.where(sub >= 4, spread, pltpu.roll(spread, 4, 0))
            level.append((value, spread))
        while len(level) > 1:
            merged = []
            for i in range(0, len(level), 2):
                (lv, la), (uv, ua) = level[i], level[i + 1]
                fv, fa = jnp.where(flips[h], uv, lv), jnp.where(flips[h], ua, la)
                bv, ba = jnp.where(flips[h], lv, uv), jnp.where(flips[h], la, ua)
                merged.append((over(fv, fa, bv), over(fa, fa, ba)))
            level = merged
        for c in range(4):
            out[c, :, pl.ds(128 * h, 128)] = level[0][0][2 * c:2 * c + 2, :]

    x_copy.wait_send()
    yh_copy.wait_send()

    def z_drain(j, carry):
        @pl.when(has_next)
        def _():
            z_copy(True, j).wait_send()

        @pl.when(has_prev)
        def _():
            z_copy(False, j).wait_send()
        return carry

    lax.fori_loop(0, 8, z_drain, 0)

    def s_drain(s, carry):
        d_copy(s).wait_send()
        pltpu.make_async_copy(ysend.at[s, pl.ds(0, 7)], ysend.at[s, pl.ds(0, 7)], y_s.at[s]).wait()
        return carry

    lax.fori_loop(0, STEPS, s_drain, 0)
    pltpu.make_async_copy(zrecv.at[pl.ds(0, 15)], zrecv.at[pl.ds(0, 15)], z_s).wait()


def local(density, bins, tf_color, tf_opacity, view_back):
    f32 = jnp.float32
    vmem = pl.BlockSpec(memory_space=pltpu.VMEM)
    hbm = pl.BlockSpec(memory_space=pltpu.HBM)
    dma = pltpu.SemaphoreType.DMA
    result = pl.pallas_call(
        kernel,
        out_shape=jax.ShapeDtypeStruct((4, 2, 256), f32),
        in_specs=[hbm] * 5,
        out_specs=vmem,
        scratch_shapes=[
            pltpu.VMEM((3, 256), jnp.bfloat16),
            pltpu.VMEM((1, 256), jnp.bfloat16),
            pltpu.VMEM((256,), jnp.int32),
            pltpu.VMEM((2, 272, 256), f32),
            pltpu.VMEM((2, 256, 256), jnp.int32),
            pltpu.VMEM((6, 256, 256), f32),
            pltpu.VMEM((2, 256, 256), f32),
            pltpu.VMEM((2, 256, 128), f32),
            pltpu.VMEM((8, 128), f32),
            pltpu.VMEM((8, 128), f32),
            pltpu.VMEM((STEPS, 2, 4, 32, 128), f32),
            pltpu.VMEM((STEPS, 4, 32, 128), f32),
            pltpu.VMEM((STEPS, 8, 2, 8, 128), f32),
            pltpu.VMEM((STEPS, 8, 2, 8, 128), f32),
            pltpu.VMEM((2 * STEPS, 8, 128), f32),
            pltpu.VMEM((16, 8, 128), f32),
            dma((5,)),
            dma((2, 8)),
            dma((2, 8)),
            dma, dma, dma, dma,
            dma((STEPS,)),
            dma((STEPS,)),
            dma((STEPS,)),
            dma((STEPS,)),
            dma, dma,
            pltpu.SemaphoreType.REGULAR,
            pltpu.SemaphoreType.REGULAR,
            pltpu.SemaphoreType.REGULAR,
        ],
        compiler_params=pltpu.CompilerParams(
            collective_id=0, has_side_effects=True, vmem_limit_bytes=60 << 20),
    )(density, bins, tf_color, tf_opacity, view_back)
    return result.reshape(4, 1, 1, 2, 256)


def solution(mesh):
    return jax.shard_map(
        local,
        mesh=mesh,
        in_specs=(P("gz", "gy", "gx"), P("gz", "gy", "gx"), P(), P(), P("gx")),
        out_specs=P(None, "gy", "gz", None, "gx"),
        check_vma=False,
    )
```

```python
import jax
import jax.numpy as jnp
from jax import lax
from jax.experimental import pallas as pl
from jax.experimental.pallas import tpu as pltpu
from jax.sharding import PartitionSpec as P

AMBIENT = 0.2
DIFFUSE = 1.6
LIGHT_X = 0.36
LIGHT_Y = 0.48
LIGHT_Z = 0.8

MESH = pl.DeviceIdType.MESH
STEPS = 8
SIB_LAG = 2
LAG = 7


def over(front, front_alpha, back):
    return front + (1.0 - front_alpha) * back


def kernel(
    density, bins, color_h, opacity_h, view_h, out,
    color, opacity, view, dens, bin_v, coef, alpha, arecv, asend, yarecv, zh, xh, xsend, xrecv, part, drecv, ysend, yrecv, zsend, zrecv,
    in_sem, zh_s, zh_r, x_s, x_r, yh_s, yh_r, d_s, d_r, y_s, y_r, z_s, z_r, a_s, a_r, ya_s, ya_r, y_ready, z_up, z_both,
):
    g = lax.axis_index("gz")
    gy = lax.axis_index("gy")
    gx = lax.axis_index("gx")
    z = lax.div(g, 16)
    y = lax.rem(lax.div(g, 2), 8)
    k = lax.rem(g, 2)
    g_prev = jnp.maximum(g - 1, 0)
    g_next = jnp.minimum(g + 1, 127)
    has_prev = g > 0
    has_next = g < 127
    sibling = g + 1 - 2 * k

    def at(zz, yy, kk):
        return ((zz * 8 + yy) * 2 + kk, gy, gx)

    barrier = pltpu.get_barrier_semaphore()

    def greet(target):
        pl.semaphore_signal(barrier, inc=1, device_id=target, device_id_type=MESH)

    def each_z(do, above):
        for j in range(1, 8):
            zz = z + j if above else z - j

            @pl.when(zz <= 7 if above else zz >= 0)
            def _():
                do(at(zz, y, k))

    pl.when(has_prev)(lambda: greet((g_prev, gy, gx)))
    pl.when(has_next)(lambda: greet((g_next, gy, gx)))
    greet((g, gy, 1 - gx))
    for j in (2, 6, 1, 7):
        greet(at(z, lax.rem(y + j, 8), k))
    greet((g, 1 - gy, gx))
    load_d = pltpu.make_async_copy(density, dens.at[:, pl.ds(8, 256), :], in_sem.at[0])
    load_b = pltpu.make_async_copy(bins, bin_v, in_sem.at[1])
    load_d.start()
    load_b.start()
    loads = [
        pltpu.make_async_copy(src, dst, in_sem.at[2 + i])
        for i, (src, dst) in enumerate(((color_h, color), (opacity_h, opacity), (view_h, view)))
    ]
    for copy in loads:
        copy.start()

    each_z(greet, True)

    @pl.when(g == 0)
    def _():
        zh[0] = jnp.zeros((256, 256), jnp.float32)

    @pl.when(g == 127)
    def _():
        zh[1] = jnp.zeros((256, 256), jnp.float32)

    zero_row = pl.multiple_of(gy * 264, 8)
    dens[:, pl.ds(zero_row, 8), :] = jnp.zeros((2, 8, 256), jnp.float32)

    lane = lax.broadcasted_iota(jnp.int32, (8, 128), 1)
    sub = lax.broadcasted_iota(jnp.int32, (8, 128), 0)

    for copy in loads:
        copy.wait()
    view_rows = view[...].reshape(1, 256)
    flips = [jnp.broadcast_to(view_rows[:, 128 * h:128 * h + 128], (8, 128)) == 1 for h in range(2)]

    load_d.wait()
    edge = pl.multiple_of((1 - gx) * 128, 128)
    packed = jnp.zeros((8, 128), jnp.float32)
    for layer in range(2):
        for t in range(32):
            i = layer * 32 + t
            tile = dens[layer, pl.ds(8 + 8 * t, 8), pl.ds(edge, 128)]
            tile = jnp.where(gx == 0, pltpu.roll(tile, i + 1, 1), pltpu.roll(tile, i, 1))
            packed = jnp.where(lane == i, tile, packed)
    xsend[...] = packed

    load_b.wait()
    tables = jnp.concatenate([color[...].astype(jnp.float32), opacity[...].astype(jnp.float32)], axis=0)
    table = [[jnp.broadcast_to(tables[c:c + 1, 128 * h:128 * h + 128], (8, 128)) for h in range(2)] for c in range(4)]

    def look(entry):
        low = jnp.bitwise_and(entry, 127)
        high = entry >= 128
        return [
            jnp.where(
                high,
                jnp.take_along_axis(table[c][1], low, axis=1, mode="promise_in_bounds"),
                jnp.take_along_axis(table[c][0], low, axis=1, mode="promise_in_bounds"),
            )
            for c in range(4)
        ]

    def lookup_block(s, carry):
        for m in range(4):
            row = pl.multiple_of(32 * s + 8 * m, 8)
            for h in range(2):
                cols = pl.ds(128 * h, 128)
                near = look(bin_v[0, pl.ds(row, 8), cols])
                far = look(bin_v[1, pl.ds(row, 8), cols])
                k_near = jnp.where(flips[h], 1.0 - far[3], 1.0) * near[3]
                k_far = jnp.where(flips[h], 1.0, 1.0 - near[3]) * far[3]
                for c in range(3):
                    coef[c, pl.ds(row, 8), cols] = k_near * near[c]
                    coef[3 + c, pl.ds(row, 8), cols] = k_far * far[c]
                alpha[h, pl.ds(row, 8), :] = near[3] + (1.0 - near[3]) * far[3]
        return carry

    lax.fori_loop(0, 8, lookup_block, 0)

    pl.semaphore_wait(
        barrier, 6 + has_prev.astype(jnp.int32) + has_next.astype(jnp.int32) + z)

    def ready(semaphore):
        return lambda target: pl.semaphore_signal(semaphore, inc=1, device_id=target, device_id_type=MESH)

    for j in (2, 6):
        ready(y_ready)(at(z, lax.rem(y + j, 8), k))

    x_copy = pltpu.make_async_remote_copy(
        src_ref=xsend, dst_ref=xrecv, send_sem=x_s, recv_sem=x_r,
        device_id=(g, gy, 1 - gx), device_id_type=MESH)
    x_copy.start()
    y_from = pl.multiple_of(jnp.where(gy == 0, 256, 8), 8)
    y_to = pl.multiple_of(jnp.where(gy == 0, 0, 264), 8)
    yh_copy = pltpu.make_async_remote_copy(
        src_ref=dens.at[:, pl.ds(y_from, 8), :], dst_ref=dens.at[:, pl.ds(y_to, 8), :],
        send_sem=yh_s, recv_sem=yh_r, device_id=(g, 1 - gy, gx), device_id_type=MESH)

    def z_copy(up, j):
        target = g_next if up else g_prev
        row = pl.multiple_of(64 * j, 64)
        slot = 0 if up else 1
        return pltpu.make_async_remote_copy(
            src_ref=dens.at[1 if up else 0, pl.ds(8 + row, 64), :],
            dst_ref=zh.at[slot, pl.ds(row, 64), :],
            send_sem=zh_s.at[slot, j], recv_sem=zh_r.at[slot, j],
            device_id=(target, gy, gx), device_id_type=MESH)

    def z_start(p, carry):
        @pl.when(has_next)
        def _():
            z_copy(True, p).start()

        @pl.when(has_prev)
        def _():
            z_copy(False, p).start()
        return carry

    lax.fori_loop(0, 1, z_start, 0)
    a_copy = pltpu.make_async_remote_copy(
        src_ref=alpha.at[1 - k], dst_ref=arecv, send_sem=a_s, recv_sem=a_r,
        device_id=(sibling, gy, gx), device_id_type=MESH)
    a_copy.start()
    yh_copy.start()
    lax.fori_loop(1, 4, z_start, 0)

    a_copy.wait_recv()

    def cut(target, s, m, at_index, value):
        target[(*at_index(2 * m),)] = value[:4]
        target[(*at_index(2 * m + 1),)] = value[4:]

    def pack_alpha(s, carry):
        for m in range(4):
            rows = pl.ds(pl.multiple_of(32 * s + 8 * m, 8), 8)
            own, sib = alpha[k, rows, :], arecv[rows, :]
            cut(asend, s, m, lambda yy: (yy, s), own + (1.0 - own) * sib)
        return carry

    lax.fori_loop(0, STEPS, pack_alpha, 0)
    yarecv[y] = asend[y]

    def ya_copy(j, late):
        yy = lax.rem(y + j, 8)
        blocks = pl.ds(4 * late, 4)
        return pltpu.make_async_remote_copy(
            src_ref=asend.at[yy, blocks], dst_ref=yarecv.at[y, blocks],
            send_sem=ya_s.at[late], recv_sem=ya_r.at[late],
            device_id=at(z, yy, k), device_id_type=MESH)

    def ya_wait(buffer, semaphore, late):
        arrived = buffer.at[pl.ds(0, 7), pl.ds(4 * late, 4)]
        pltpu.make_async_copy(arrived, arrived, semaphore.at[late]).wait()

    for late in range(2):
        for j in (2, 6, 1, 7):
            ya_copy(j, late).start()
    each_z(ready(z_up), False)

    x_copy.wait_recv()
    columns = xrecv[...]
    for layer in range(2):
        for t in range(32):
            i = layer * 32 + t
            xh[layer, pl.ds(8 * t, 8), :] = jnp.broadcast_to(columns[:, i:i + 1], (8, 128))

    def wait_z(s):
        base = pl.multiple_of(64 * s, 64)
        for slot, there in ((0, has_prev), (1, has_next)):
            @pl.when(there)
            def _():
                pltpu.make_async_copy(
                    zh.at[slot, pl.ds(base, 64), :], zh.at[slot, pl.ds(base, 64), :], zh_r.at[slot, s]).wait()

    def shade_block(s):
        base = pl.multiple_of(32 * s, 32)
        tiles = [[[dens[layer, pl.ds(pl.multiple_of(base + 8 * t, 8), 8), pl.ds(128 * h, 128)] for h in range(2)]
                  for t in range(6)] for layer in range(2)]
        for m in range(4):
            row = pl.multiple_of(base + 8 * m, 8)
            shades = []
            for layer in range(2):
                before, here, after = tiles[layer][m], tiles[layer][m + 1], tiles[layer][m + 2]
                side = xh[layer, pl.ds(row, 8), :]
                ends = [jnp.where(gx == 1, side, 0.0), jnp.where(gx == 0, side, 0.0)]
                to_right = [pltpu.roll(here[h], 1, 1) for h in range(2)]
                to_left = [pltpu.roll(here[h], 127, 1) for h in range(2)]
                left = [jnp.where(lane == 0, ends[0], to_right[0]), jnp.where(lane == 0, to_right[0], to_right[1])]
                right = [jnp.where(lane == 127, to_left[1], to_left[0]), jnp.where(lane == 127, ends[1], to_left[1])]
                for h in range(2):
                    cols = pl.ds(128 * h, 128)
                    above = jnp.where(sub == 0, pltpu.roll(before[h], 1, 0), pltpu.roll(here[h], 1, 0))
                    below = jnp.where(sub == 7, pltpu.roll(after[h], 7, 0), pltpu.roll(here[h], 7, 0))
                    other = tiles[1 - layer][m + 1][h]
                    if layer == 0:
                        dz = other - zh[0, pl.ds(row, 8), cols]
                    else:
                        dz = zh[1, pl.ds(row, 8), cols] - other
                    dx = right[h] - left[h]
                    dy = below - above
                    dot = dx * (0.5 * DIFFUSE * LIGHT_X) + dy * (0.5 * DIFFUSE * LIGHT_Y) + dz * (0.5 * DIFFUSE * LIGHT_Z)
                    norm = 1.0 + 0.25 * (dx * dx + dy * dy + dz * dz)
                    shades.append(AMBIENT + jnp.abs(dot) * lax.rsqrt(norm))
            for h in range(2):
                cols = pl.ds(128 * h, 128)
                for c in range(3):
                    part[s, h, c, pl.ds(8 * m, 8), :] = (
                        coef[c, pl.ds(row, 8), cols] * shades[h] + coef[3 + c, pl.ds(row, 8), cols] * shades[2 + h])

    def d_copy(s):
        return pltpu.make_async_remote_copy(
            src_ref=part.at[s, 1 - k], dst_ref=drecv.at[s], send_sem=d_s.at[s], recv_sem=d_r.at[s],
            device_id=(sibling, gy, gx), device_id_type=MESH)

    flip = jnp.where(k == 0, flips[0].astype(jnp.int32), flips[1].astype(jnp.int32)) == 1
    own_front = jnp.where(flip, 1, 0) == k

    def y_copy(u, first, count, yy):
        blocks = pl.ds(first, count)
        return pltpu.make_async_remote_copy(
            src_ref=ysend.at[yy, blocks], dst_ref=yrecv.at[y, blocks], send_sem=y_s.at[u], recv_sem=y_r.at[u],
            device_id=at(z, yy, k), device_id_type=MESH)

    def y_start(u, first, count):
        for j in (4, 3, 5, 2, 6, 1, 7):
            y_copy(u, first, count, lax.rem(y + j, 8)).start()

    def y_wait(buffer, semaphore, u, first, count):
        arrived = buffer.at[pl.ds(0, 7), pl.ds(first, count)]
        pltpu.make_async_copy(arrived, arrived, semaphore.at[u]).wait()

    def merge_pack(s):
        d_copy(s).wait_recv()
        for m in range(4):
            rows = pl.ds(8 * m, 8)
            whole = pl.ds(pl.multiple_of(32 * s + 8 * m, 8), 8)
            through = 1.0 - jnp.where(own_front, alpha[k, whole, :], arecv[whole, :])
            for c in range(3):
                own, sib = part[s, k, c, rows, :], drecv[s, c, rows, :]
                merged = jnp.where(own_front, own, sib) + through * jnp.where(own_front, sib, own)
                cut(ysend, s, m, lambda yy: (yy, s, c), merged)
        yrecv[y, s] = ysend[y, s]

        @pl.when(s < 2)
        def _():
            y_start(s, s, 1)

        @pl.when(jnp.logical_and(s >= 2, lax.rem(s, 2) == 1))
        def _():
            y_start(lax.div(s + 3, 2) - 1, s - 1, 2)

    flip4 = flip[:4]

    def weigh(s):
        alphas = [yarecv[i, s] for i in range(8)]
        through = [1.0 - a for a in alphas]
        before, after = [jnp.ones((4, 128), jnp.float32)], [jnp.ones((4, 128), jnp.float32)]
        for i in range(7):
            before.append(before[-1] * through[i])
            after.append(after[-1] * through[7 - i])
        while len(alphas) > 1:
            alphas = [alphas[i] + (1.0 - alphas[i]) * alphas[i + 1] for i in range(0, len(alphas), 2)]
        return [jnp.where(flip4, after[7 - i], before[i]) for i in range(8)], alphas[0]

    def z_send(s):
        @pl.when(s == 0)
        def _():
            ya_wait(yarecv, ya_r, 0)

        @pl.when(s == 4)
        def _():
            ya_wait(yarecv, ya_r, 1)

        weights, whole = weigh(s)

        @pl.when(s < 2)
        def _():
            y_wait(yrecv, y_r, s, s, 1)

        @pl.when(jnp.logical_and(s >= 2, lax.rem(s, 2) == 0))
        def _():
            y_wait(yrecv, y_r, lax.div(s, 2) + 1, s, 2)

        total = []
        for c in range(3):
            terms = [weights[i] * yrecv[i, s, c] for i in range(8)]
            while len(terms) > 1:
                terms = [terms[i] + terms[i + 1] for i in range(0, len(terms), 2)]
            total.append(terms[0])
        total.append(whole)
        for kk in range(2):
            piece = jnp.concatenate([t[2 * kk:2 * kk + 2] for t in total], axis=0)
            zsend[2 * s + kk] = piece
            mine = jnp.logical_and(s == z, k == kk)

            @pl.when(mine)
            def _():
                zrecv[2 * z + k] = piece

            @pl.when(jnp.logical_not(mine))
            def _():
                pltpu.make_async_remote_copy(
                    src_ref=zsend.at[2 * s + kk], dst_ref=zrecv.at[2 * z + k], send_sem=z_s, recv_sem=z_r,
                    device_id=at(s, y, kk), device_id_type=MESH).start()

    def step(s, carry):
        @pl.when(s == jnp.where(gy == 1, 0, STEPS - 1))
        def _():
            yh_copy.wait_recv()

        @pl.when(jnp.logical_and(s < STEPS, lax.rem(s, 2) == 0))
        def _():
            wait_z(lax.div(s, 2))

        @pl.when(s < STEPS)
        def _():
            shade_block(s)
            d_copy(s).start()

        @pl.when(s == 0)
        def _():
            pl.semaphore_wait(y_ready, 2)
            for j in (4, 3, 5):
                ya_copy(j, 0).start()

        @pl.when(jnp.logical_and(s >= SIB_LAG, s < STEPS + SIB_LAG))
        def _():
            merge_pack(s - SIB_LAG)

        @pl.when(s == SIB_LAG + 3)
        def _():
            for j in (4, 3, 5):
                ya_copy(j, 1).start()

        @pl.when(s == LAG - 1)
        def _():
            @pl.when(z < 7)
            def _():
                pl.semaphore_wait(z_up, 7 - z)
            ready(z_both)((sibling, gy, gx))

        @pl.when(s == LAG)
        def _():
            pl.semaphore_wait(z_both, 1)

        @pl.when(s >= LAG)
        def _():
            z_send(s - LAG)
        return carry

    lax.fori_loop(0, STEPS + LAG, step, 0)

    pltpu.make_async_copy(zrecv.at[pl.ds(0, 15)], zrecv.at[pl.ds(0, 15)], z_r).wait()
    for h in range(2):
        level = []
        for i in range(8):
            value = zrecv[2 * i + h]
            spread = jnp.where(sub >= 6, value, pltpu.roll(value, 6, 0))
            spread = jnp.where(sub >= 4, spread, pltpu.roll(spread, 4, 0))
            level.append((value, spread))
        while len(level) > 1:
            merged = []
            for i in range(0, len(level), 2):
                (lv, la), (uv, ua) = level[i], level[i + 1]
                fv, fa = jnp.where(flips[h], uv, lv), jnp.where(flips[h], ua, la)
                bv, ba = jnp.where(flips[h], lv, uv), jnp.where(flips[h], la, ua)
                merged.append((over(fv, fa, bv), over(fa, fa, ba)))
            level = merged
        for c in range(4):
            out[c, :, pl.ds(128 * h, 128)] = level[0][0][2 * c:2 * c + 2, :]

    x_copy.wait_send()
    yh_copy.wait_send()

    def z_drain(j, carry):
        @pl.when(has_next)
        def _():
            z_copy(True, j).wait_send()

        @pl.when(has_prev)
        def _():
            z_copy(False, j).wait_send()
        return carry

    lax.fori_loop(0, 4, z_drain, 0)
    a_copy.wait_send()
    for late in range(2):
        ya_wait(asend, ya_s, late)

    def s_drain(s, carry):
        d_copy(s).wait_send()
        return carry

    lax.fori_loop(0, STEPS, s_drain, 0)
    for u, (first, count) in enumerate(((0, 1), (1, 1), (2, 2), (4, 2), (6, 2))):
        y_wait(ysend, y_s, u, first, count)
    pltpu.make_async_copy(zrecv.at[pl.ds(0, 15)], zrecv.at[pl.ds(0, 15)], z_s).wait()


def local(density, bins, tf_color, tf_opacity, view_back):
    f32 = jnp.float32
    vmem = pl.BlockSpec(memory_space=pltpu.VMEM)
    hbm = pl.BlockSpec(memory_space=pltpu.HBM)
    dma = pltpu.SemaphoreType.DMA
    result = pl.pallas_call(
        kernel,
        out_shape=jax.ShapeDtypeStruct((4, 2, 256), f32),
        in_specs=[hbm] * 5,
        out_specs=vmem,
        scratch_shapes=[
            pltpu.VMEM((3, 256), jnp.bfloat16),
            pltpu.VMEM((1, 256), jnp.bfloat16),
            pltpu.VMEM((256,), jnp.int32),
            pltpu.VMEM((2, 272, 256), f32),
            pltpu.VMEM((2, 256, 256), jnp.int32),
            pltpu.VMEM((6, 256, 256), f32),
            pltpu.VMEM((2, 256, 128), f32),
            pltpu.VMEM((256, 128), f32),
            pltpu.VMEM((8, STEPS, 4, 128), f32),
            pltpu.VMEM((8, STEPS, 4, 128), f32),
            pltpu.VMEM((2, 256, 256), f32),
            pltpu.VMEM((2, 256, 128), f32),
            pltpu.VMEM((8, 128), f32),
            pltpu.VMEM((8, 128), f32),
            pltpu.VMEM((STEPS, 2, 3, 32, 128), f32),
            pltpu.VMEM((STEPS, 3, 32, 128), f32),
            pltpu.VMEM((8, STEPS, 3, 4, 128), f32),
            pltpu.VMEM((8, STEPS, 3, 4, 128), f32),
            pltpu.VMEM((2 * STEPS, 8, 128), f32),
            pltpu.VMEM((16, 8, 128), f32),
            dma((5,)),
            dma((2, 4)),
            dma((2, 4)),
            dma, dma, dma, dma,
            dma((STEPS,)),
            dma((STEPS,)),
            dma((STEPS,)),
            dma((STEPS,)),
            dma, dma, dma, dma,
            dma((2,)),
            dma((2,)),
            pltpu.SemaphoreType.REGULAR,
            pltpu.SemaphoreType.REGULAR,
            pltpu.SemaphoreType.REGULAR,
        ],
        compiler_params=pltpu.CompilerParams(
            collective_id=0, has_side_effects=True, vmem_limit_bytes=60 << 20),
    )(density, bins, tf_color, tf_opacity, view_back)
    return result.reshape(4, 1, 1, 2, 256)


def solution(mesh):
    return jax.shard_map(
        local,
        mesh=mesh,
        in_specs=(P("gz", "gy", "gx"), P("gz", "gy", "gx"), P(), P(), P("gx")),
        out_specs=P(None, "gy", "gz", None, "gx"),
        check_vma=False,
    )
```

```python
import jax
import jax.numpy as jnp
from jax import lax
from jax.experimental import pallas as pl
from jax.experimental.pallas import tpu as pltpu
from jax.sharding import PartitionSpec as P

AMBIENT = 0.2
DIFFUSE = 1.6
LIGHT_X = 0.36
LIGHT_Y = 0.48
LIGHT_Z = 0.8

MESH = pl.DeviceIdType.MESH
STEPS = 8
SENDS = ((0, 1), (1, 1), (2, 1), (3, 1), (4, 2), (6, 2))
SIB_LAG = 2
LAG = 7


def over(front, front_alpha, back):
    return front + (1.0 - front_alpha) * back


def kernel(
    density, bins, color_h, opacity_h, view_h, out,
    color, opacity, view, dens, bin_v, coef, alpha, arecv, asend, yarecv, zh, xh, xsend, xrecv, part, drecv, ysend, yrecv, zsend, zrecv,
    in_sem, zh_s, zh_r, x_s, x_r, yh_s, yh_r, d_s, d_r, y_s, y_r, z_s, z_r, a_s, a_r, ya_s, ya_r, y_ready, z_up, z_both,
):
    g = lax.axis_index("gz")
    gy = lax.axis_index("gy")
    gx = lax.axis_index("gx")
    z = lax.div(g, 16)
    y = lax.rem(lax.div(g, 2), 8)
    k = lax.rem(g, 2)
    g_prev = jnp.maximum(g - 1, 0)
    g_next = jnp.minimum(g + 1, 127)
    has_prev = g > 0
    has_next = g < 127
    sibling = g + 1 - 2 * k

    def at(zz, yy, kk):
        return ((zz * 8 + yy) * 2 + kk, gy, gx)

    barrier = pltpu.get_barrier_semaphore()

    def greet(target):
        pl.semaphore_signal(barrier, inc=1, device_id=target, device_id_type=MESH)

    def each_z(do, above):
        for j in range(1, 8):
            zz = z + j if above else z - j

            @pl.when(zz <= 7 if above else zz >= 0)
            def _():
                do(at(zz, y, k))

    pl.when(has_prev)(lambda: greet((g_prev, gy, gx)))
    pl.when(has_next)(lambda: greet((g_next, gy, gx)))
    greet((g, gy, 1 - gx))
    for j in (2, 6, 1, 7):
        greet(at(z, lax.rem(y + j, 8), k))
    greet((g, 1 - gy, gx))
    load_d = pltpu.make_async_copy(density, dens.at[:, pl.ds(8, 256), :], in_sem.at[0])
    load_b = pltpu.make_async_copy(bins, bin_v, in_sem.at[1])
    load_d.start()
    load_b.start()
    loads = [
        pltpu.make_async_copy(src, dst, in_sem.at[2 + i])
        for i, (src, dst) in enumerate(((color_h, color), (opacity_h, opacity), (view_h, view)))
    ]
    for copy in loads:
        copy.start()

    each_z(greet, True)

    @pl.when(g == 0)
    def _():
        zh[0] = jnp.zeros((256, 256), jnp.float32)

    @pl.when(g == 127)
    def _():
        zh[1] = jnp.zeros((256, 256), jnp.float32)

    zero_row = pl.multiple_of(gy * 264, 8)
    dens[:, pl.ds(zero_row, 8), :] = jnp.zeros((2, 8, 256), jnp.float32)

    lane = lax.broadcasted_iota(jnp.int32, (8, 128), 1)
    sub = lax.broadcasted_iota(jnp.int32, (8, 128), 0)

    for copy in loads:
        copy.wait()
    view_rows = view[...].reshape(1, 256)
    flips = [jnp.broadcast_to(view_rows[:, 128 * h:128 * h + 128], (8, 128)) == 1 for h in range(2)]

    load_d.wait()
    edge = pl.multiple_of((1 - gx) * 128, 128)
    packed = jnp.zeros((8, 128), jnp.float32)
    for layer in range(2):
        for t in range(32):
            i = layer * 32 + t
            tile = dens[layer, pl.ds(8 + 8 * t, 8), pl.ds(edge, 128)]
            tile = jnp.where(gx == 0, pltpu.roll(tile, i + 1, 1), pltpu.roll(tile, i, 1))
            packed = jnp.where(lane == i, tile, packed)
    xsend[...] = packed

    load_b.wait()
    tables = jnp.concatenate([color[...].astype(jnp.float32), opacity[...].astype(jnp.float32)], axis=0)
    table = [[jnp.broadcast_to(tables[c:c + 1, 128 * h:128 * h + 128], (8, 128)) for h in range(2)] for c in range(4)]

    def look(entry):
        low = jnp.bitwise_and(entry, 127)
        high = entry >= 128
        return [
            jnp.where(
                high,
                jnp.take_along_axis(table[c][1], low, axis=1, mode="promise_in_bounds"),
                jnp.take_along_axis(table[c][0], low, axis=1, mode="promise_in_bounds"),
            )
            for c in range(4)
        ]

    def lookup_block(s, carry):
        for m in range(4):
            row = pl.multiple_of(32 * s + 8 * m, 8)
            for h in range(2):
                cols = pl.ds(128 * h, 128)
                near = look(bin_v[0, pl.ds(row, 8), cols])
                far = look(bin_v[1, pl.ds(row, 8), cols])
                k_near = jnp.where(flips[h], 1.0 - far[3], 1.0) * near[3]
                k_far = jnp.where(flips[h], 1.0, 1.0 - near[3]) * far[3]
                for c in range(3):
                    coef[c, pl.ds(row, 8), cols] = k_near * near[c]
                    coef[3 + c, pl.ds(row, 8), cols] = k_far * far[c]
                alpha[h, pl.ds(row, 8), :] = near[3] + (1.0 - near[3]) * far[3]
        return carry

    pl.semaphore_wait(
        barrier, 6 + has_prev.astype(jnp.int32) + has_next.astype(jnp.int32) + z)


    def ready(semaphore):
        return lambda target: pl.semaphore_signal(semaphore, inc=1, device_id=target, device_id_type=MESH)

    for j in (2, 6):
        ready(y_ready)(at(z, lax.rem(y + j, 8), k))

    x_copy = pltpu.make_async_remote_copy(
        src_ref=xsend, dst_ref=xrecv, send_sem=x_s, recv_sem=x_r,
        device_id=(g, gy, 1 - gx), device_id_type=MESH)
    x_copy.start()
    y_from = pl.multiple_of(jnp.where(gy == 0, 256, 8), 8)
    y_to = pl.multiple_of(jnp.where(gy == 0, 0, 264), 8)
    yh_copy = pltpu.make_async_remote_copy(
        src_ref=dens.at[:, pl.ds(y_from, 8), :], dst_ref=dens.at[:, pl.ds(y_to, 8), :],
        send_sem=yh_s, recv_sem=yh_r, device_id=(g, 1 - gy, gx), device_id_type=MESH)

    def z_copy(up, j):
        target = g_next if up else g_prev
        row = pl.multiple_of(64 * j, 64)
        slot = 0 if up else 1
        return pltpu.make_async_remote_copy(
            src_ref=dens.at[1 if up else 0, pl.ds(8 + row, 64), :],
            dst_ref=zh.at[slot, pl.ds(row, 64), :],
            send_sem=zh_s.at[slot, j], recv_sem=zh_r.at[slot, j],
            device_id=(target, gy, gx), device_id_type=MESH)

    def z_start(p, carry):
        @pl.when(has_next)
        def _():
            z_copy(True, p).start()

        @pl.when(has_prev)
        def _():
            z_copy(False, p).start()
        return carry

    lax.fori_loop(0, 1, z_start, 0)
    yh_copy.start()
    lax.fori_loop(1, 4, z_start, 0)
    lax.fori_loop(0, 8, lookup_block, 0)
    a_copy = pltpu.make_async_remote_copy(
        src_ref=alpha.at[1 - k], dst_ref=arecv, send_sem=a_s, recv_sem=a_r,
        device_id=(sibling, gy, gx), device_id_type=MESH)
    a_copy.start()

    def cut(target, s, m, at_index, value):
        target[(*at_index(2 * m),)] = value[:4]
        target[(*at_index(2 * m + 1),)] = value[4:]

    def pack_alpha(s, carry):
        for m in range(4):
            rows = pl.ds(pl.multiple_of(32 * s + 8 * m, 8), 8)
            own, sib = alpha[k, rows, :], arecv[rows, :]
            cut(asend, s, m, lambda yy: (yy, s), own + (1.0 - own) * sib)
        return carry

    def ya_copy(j, late):
        yy = lax.rem(y + j, 8)
        blocks = pl.ds(4 * late, 4)
        return pltpu.make_async_remote_copy(
            src_ref=asend.at[yy, blocks], dst_ref=yarecv.at[y, blocks],
            send_sem=ya_s.at[late], recv_sem=ya_r.at[late],
            device_id=at(z, yy, k), device_id_type=MESH)

    def ya_wait(buffer, semaphore, late):
        arrived = buffer.at[pl.ds(0, 7), pl.ds(4 * late, 4)]
        pltpu.make_async_copy(arrived, arrived, semaphore.at[late]).wait()

    each_z(ready(z_up), False)

    x_copy.wait_recv()
    columns = xrecv[...]
    for layer in range(2):
        for t in range(32):
            i = layer * 32 + t
            xh[layer, pl.ds(8 * t, 8), :] = jnp.broadcast_to(columns[:, i:i + 1], (8, 128))

    def wait_z(s):
        base = pl.multiple_of(64 * s, 64)
        for slot, there in ((0, has_prev), (1, has_next)):
            @pl.when(there)
            def _():
                pltpu.make_async_copy(
                    zh.at[slot, pl.ds(base, 64), :], zh.at[slot, pl.ds(base, 64), :], zh_r.at[slot, s]).wait()

    def shade_block(s):
        base = pl.multiple_of(32 * s, 32)
        tiles = [[[dens[layer, pl.ds(pl.multiple_of(base + 8 * t, 8), 8), pl.ds(128 * h, 128)] for h in range(2)]
                  for t in range(6)] for layer in range(2)]
        for m in range(4):
            row = pl.multiple_of(base + 8 * m, 8)
            shades = []
            for layer in range(2):
                before, here, after = tiles[layer][m], tiles[layer][m + 1], tiles[layer][m + 2]
                side = xh[layer, pl.ds(row, 8), :]
                ends = [jnp.where(gx == 1, side, 0.0), jnp.where(gx == 0, side, 0.0)]
                to_right = [pltpu.roll(here[h], 1, 1) for h in range(2)]
                to_left = [pltpu.roll(here[h], 127, 1) for h in range(2)]
                left = [jnp.where(lane == 0, ends[0], to_right[0]), jnp.where(lane == 0, to_right[0], to_right[1])]
                right = [jnp.where(lane == 127, to_left[1], to_left[0]), jnp.where(lane == 127, ends[1], to_left[1])]
                for h in range(2):
                    cols = pl.ds(128 * h, 128)
                    above = jnp.where(sub == 0, pltpu.roll(before[h], 1, 0), pltpu.roll(here[h], 1, 0))
                    below = jnp.where(sub == 7, pltpu.roll(after[h], 7, 0), pltpu.roll(here[h], 7, 0))
                    other = tiles[1 - layer][m + 1][h]
                    if layer == 0:
                        dz = other - zh[0, pl.ds(row, 8), cols]
                    else:
                        dz = zh[1, pl.ds(row, 8), cols] - other
                    dx = right[h] - left[h]
                    dy = below - above
                    dot = dx * (0.5 * DIFFUSE * LIGHT_X) + dy * (0.5 * DIFFUSE * LIGHT_Y) + dz * (0.5 * DIFFUSE * LIGHT_Z)
                    norm = 1.0 + 0.25 * (dx * dx + dy * dy + dz * dz)
                    shades.append(AMBIENT + jnp.abs(dot) * lax.rsqrt(norm))
            for h in range(2):
                cols = pl.ds(128 * h, 128)
                for c in range(3):
                    part[s, h, c, pl.ds(8 * m, 8), :] = (
                        coef[c, pl.ds(row, 8), cols] * shades[h] + coef[3 + c, pl.ds(row, 8), cols] * shades[2 + h])

    def d_copy(s):
        return pltpu.make_async_remote_copy(
            src_ref=part.at[s, 1 - k], dst_ref=drecv.at[s], send_sem=d_s.at[s], recv_sem=d_r.at[s],
            device_id=(sibling, gy, gx), device_id_type=MESH)

    flip = jnp.where(k == 0, flips[0].astype(jnp.int32), flips[1].astype(jnp.int32)) == 1
    own_front = jnp.where(flip, 1, 0) == k

    def y_copy(u, first, count, yy):
        blocks = pl.ds(first, count)
        return pltpu.make_async_remote_copy(
            src_ref=ysend.at[yy, blocks], dst_ref=yrecv.at[y, blocks], send_sem=y_s.at[u], recv_sem=y_r.at[u],
            device_id=at(z, yy, k), device_id_type=MESH)

    def y_start(u, first, count):
        for j in (4, 3, 5, 2, 6, 1, 7):
            y_copy(u, first, count, lax.rem(y + j, 8)).start()

    def y_wait(buffer, semaphore, u, first, count):
        arrived = buffer.at[pl.ds(0, 7), pl.ds(first, count)]
        pltpu.make_async_copy(arrived, arrived, semaphore.at[u]).wait()

    def merge_pack(s):
        d_copy(s).wait_recv()
        for m in range(4):
            rows = pl.ds(8 * m, 8)
            whole = pl.ds(pl.multiple_of(32 * s + 8 * m, 8), 8)
            through = 1.0 - jnp.where(own_front, alpha[k, whole, :], arecv[whole, :])
            for c in range(3):
                own, sib = part[s, k, c, rows, :], drecv[s, c, rows, :]
                merged = jnp.where(own_front, own, sib) + through * jnp.where(own_front, sib, own)
                cut(ysend, s, m, lambda yy: (yy, s, c), merged)
        yrecv[y, s] = ysend[y, s]

        for u, (first, count) in enumerate(SENDS):
            @pl.when(s == first + count - 1)
            def _():
                y_start(u, first, count)

    flip4 = flip[:4]

    def weigh(s):
        alphas = [yarecv[i, s] for i in range(8)]
        through = [1.0 - a for a in alphas]
        before, after = [jnp.ones((4, 128), jnp.float32)], [jnp.ones((4, 128), jnp.float32)]
        for i in range(7):
            before.append(before[-1] * through[i])
            after.append(after[-1] * through[7 - i])
        while len(alphas) > 1:
            alphas = [alphas[i] + (1.0 - alphas[i]) * alphas[i + 1] for i in range(0, len(alphas), 2)]
        return [jnp.where(flip4, after[7 - i], before[i]) for i in range(8)], alphas[0]

    def z_send(s):
        @pl.when(s == 0)
        def _():
            ya_wait(yarecv, ya_r, 0)

        @pl.when(s == 4)
        def _():
            ya_wait(yarecv, ya_r, 1)

        weights, whole = weigh(s)

        for u, (first, count) in enumerate(SENDS):
            @pl.when(s == first)
            def _():
                y_wait(yrecv, y_r, u, first, count)

        total = []
        for c in range(3):
            terms = [weights[i] * yrecv[i, s, c] for i in range(8)]
            while len(terms) > 1:
                terms = [terms[i] + terms[i + 1] for i in range(0, len(terms), 2)]
            total.append(terms[0])
        total.append(whole)
        for kk in range(2):
            piece = jnp.concatenate([t[2 * kk:2 * kk + 2] for t in total], axis=0)
            zsend[2 * s + kk] = piece
            mine = jnp.logical_and(s == z, k == kk)

            @pl.when(mine)
            def _():
                zrecv[2 * z + k] = piece

            @pl.when(jnp.logical_not(mine))
            def _():
                pltpu.make_async_remote_copy(
                    src_ref=zsend.at[2 * s + kk], dst_ref=zrecv.at[2 * z + k], send_sem=z_s, recv_sem=z_r,
                    device_id=at(s, y, kk), device_id_type=MESH).start()

    def step(s, carry):
        @pl.when(s == jnp.where(gy == 1, 0, STEPS - 1))
        def _():
            yh_copy.wait_recv()

        @pl.when(jnp.logical_and(s < STEPS, lax.rem(s, 2) == 0))
        def _():
            wait_z(lax.div(s, 2))

        @pl.when(s < STEPS)
        def _():
            shade_block(s)
            d_copy(s).start()

        @pl.when(s == 0)
        def _():
            a_copy.wait_recv()
            lax.fori_loop(0, STEPS, pack_alpha, 0)
            yarecv[y] = asend[y]
            for j in (2, 6, 1, 7):
                ya_copy(j, 0).start()
            pl.semaphore_wait(y_ready, 2)
            for j in (4, 3, 5):
                ya_copy(j, 0).start()
            for j in (2, 6, 1, 7):
                ya_copy(j, 1).start()

        @pl.when(jnp.logical_and(s >= SIB_LAG, s < STEPS + SIB_LAG))
        def _():
            merge_pack(s - SIB_LAG)

        @pl.when(s == SIB_LAG + 3)
        def _():
            for j in (4, 3, 5):
                ya_copy(j, 1).start()

        @pl.when(s == LAG - 1)
        def _():
            @pl.when(z < 7)
            def _():
                pl.semaphore_wait(z_up, 7 - z)
            ready(z_both)((sibling, gy, gx))

        @pl.when(s == LAG)
        def _():
            pl.semaphore_wait(z_both, 1)

        @pl.when(s >= LAG)
        def _():
            z_send(s - LAG)
        return carry

    lax.fori_loop(0, STEPS + LAG, step, 0)

    pltpu.make_async_copy(zrecv.at[pl.ds(0, 15)], zrecv.at[pl.ds(0, 15)], z_r).wait()
    for h in range(2):
        level = []
        for i in range(8):
            value = zrecv[2 * i + h]
            spread = jnp.where(sub >= 6, value, pltpu.roll(value, 6, 0))
            spread = jnp.where(sub >= 4, spread, pltpu.roll(spread, 4, 0))
            level.append((value, spread))
        while len(level) > 1:
            merged = []
            for i in range(0, len(level), 2):
                (lv, la), (uv, ua) = level[i], level[i + 1]
                fv, fa = jnp.where(flips[h], uv, lv), jnp.where(flips[h], ua, la)
                bv, ba = jnp.where(flips[h], lv, uv), jnp.where(flips[h], la, ua)
                merged.append((over(fv, fa, bv), over(fa, fa, ba)))
            level = merged
        for c in range(4):
            out[c, :, pl.ds(128 * h, 128)] = level[0][0][2 * c:2 * c + 2, :]

    x_copy.wait_send()
    yh_copy.wait_send()

    def z_drain(j, carry):
        @pl.when(has_next)
        def _():
            z_copy(True, j).wait_send()

        @pl.when(has_prev)
        def _():
            z_copy(False, j).wait_send()
        return carry

    lax.fori_loop(0, 4, z_drain, 0)
    a_copy.wait_send()
    for late in range(2):
        ya_wait(asend, ya_s, late)

    def s_drain(s, carry):
        d_copy(s).wait_send()
        return carry

    lax.fori_loop(0, STEPS, s_drain, 0)
    for u, (first, count) in enumerate(SENDS):
        y_wait(ysend, y_s, u, first, count)
    pltpu.make_async_copy(zrecv.at[pl.ds(0, 15)], zrecv.at[pl.ds(0, 15)], z_s).wait()


def local(density, bins, tf_color, tf_opacity, view_back):
    f32 = jnp.float32
    vmem = pl.BlockSpec(memory_space=pltpu.VMEM)
    hbm = pl.BlockSpec(memory_space=pltpu.HBM)
    dma = pltpu.SemaphoreType.DMA
    result = pl.pallas_call(
        kernel,
        out_shape=jax.ShapeDtypeStruct((4, 2, 256), f32),
        in_specs=[hbm] * 5,
        out_specs=vmem,
        scratch_shapes=[
            pltpu.VMEM((3, 256), jnp.bfloat16),
            pltpu.VMEM((1, 256), jnp.bfloat16),
            pltpu.VMEM((256,), jnp.int32),
            pltpu.VMEM((2, 272, 256), f32),
            pltpu.VMEM((2, 256, 256), jnp.int32),
            pltpu.VMEM((6, 256, 256), f32),
            pltpu.VMEM((2, 256, 128), f32),
            pltpu.VMEM((256, 128), f32),
            pltpu.VMEM((8, STEPS, 4, 128), f32),
            pltpu.VMEM((8, STEPS, 4, 128), f32),
            pltpu.VMEM((2, 256, 256), f32),
            pltpu.VMEM((2, 256, 128), f32),
            pltpu.VMEM((8, 128), f32),
            pltpu.VMEM((8, 128), f32),
            pltpu.VMEM((STEPS, 2, 3, 32, 128), f32),
            pltpu.VMEM((STEPS, 3, 32, 128), f32),
            pltpu.VMEM((8, STEPS, 3, 4, 128), f32),
            pltpu.VMEM((8, STEPS, 3, 4, 128), f32),
            pltpu.VMEM((2 * STEPS, 8, 128), f32),
            pltpu.VMEM((16, 8, 128), f32),
            dma((5,)),
            dma((2, 4)),
            dma((2, 4)),
            dma, dma, dma, dma,
            dma((STEPS,)),
            dma((STEPS,)),
            dma((STEPS,)),
            dma((STEPS,)),
            dma, dma, dma, dma,
            dma((2,)),
            dma((2,)),
            pltpu.SemaphoreType.REGULAR,
            pltpu.SemaphoreType.REGULAR,
            pltpu.SemaphoreType.REGULAR,
        ],
        compiler_params=pltpu.CompilerParams(
            collective_id=0, has_side_effects=True, vmem_limit_bytes=60 << 20),
    )(density, bins, tf_color, tf_opacity, view_back)
    return result.reshape(4, 1, 1, 2, 256)


def solution(mesh):
    return jax.shard_map(
        local,
        mesh=mesh,
        in_specs=(P("gz", "gy", "gx"), P("gz", "gy", "gx"), P(), P(), P("gx")),
        out_specs=P(None, "gy", "gz", None, "gx"),
        check_vma=False,
    )
```

```python
import jax
import jax.numpy as jnp
from jax import lax
from jax.experimental import pallas as pl
from jax.experimental.pallas import tpu as pltpu
from jax.sharding import PartitionSpec as P

AMBIENT = 0.2
DIFFUSE = 1.6
LIGHT_X = 0.36
LIGHT_Y = 0.48
LIGHT_Z = 0.8

MESH = pl.DeviceIdType.MESH
STEPS = 8
Z_GROUPS = ((0, 1), (1, 1), (2, 2), (4, 4))
SENDS = ((0, 1), (1, 1), (2, 1), (3, 1), (4, 2), (6, 2))
SIB_LAG = 2
LAG = 7


def over(front, front_alpha, back):
    return front + (1.0 - front_alpha) * back


def kernel(
    density, bins, color_h, opacity_h, view_h, out,
    color, opacity, view, dens, bin_v, coef, alpha, arecv, asend, yarecv, zh, xh, xsend, xrecv, part, drecv, ysend, yrecv, zsend, zrecv,
    in_sem, zh_s, zh_r, x_s, x_r, yh_s, yh_r, d_s, d_r, y_s, y_r, z_s, z_r, a_s, a_r, ya_s, ya_r, y_ready, z_up, z_both,
):
    g = lax.axis_index("gz")
    gy = lax.axis_index("gy")
    gx = lax.axis_index("gx")
    z = lax.div(g, 16)
    y = lax.rem(lax.div(g, 2), 8)
    k = lax.rem(g, 2)
    g_prev = jnp.maximum(g - 1, 0)
    g_next = jnp.minimum(g + 1, 127)
    has_prev = g > 0
    has_next = g < 127
    sibling = g + 1 - 2 * k

    def at(zz, yy, kk):
        return ((zz * 8 + yy) * 2 + kk, gy, gx)

    load_d = pltpu.make_async_copy(density, dens.at[:, pl.ds(8, 256), :], in_sem.at[0])
    load_d.start()
    barrier = pltpu.get_barrier_semaphore()

    def greet(target):
        pl.semaphore_signal(barrier, inc=1, device_id=target, device_id_type=MESH)

    def each_z(do, above):
        for j in range(1, 8):
            zz = z + j if above else z - j

            @pl.when(zz <= 7 if above else zz >= 0)
            def _():
                do(at(zz, y, k))

    greet((g, 1 - gy, gx))
    pl.when(has_prev)(lambda: greet((g_prev, gy, gx)))
    pl.when(has_next)(lambda: greet((g_next, gy, gx)))
    greet((g, gy, 1 - gx))
    for j in (2, 6, 1, 7):
        greet(at(z, lax.rem(y + j, 8), k))
    load_b = pltpu.make_async_copy(bins, bin_v, in_sem.at[1])
    load_b.start()
    loads = [
        pltpu.make_async_copy(src, dst, in_sem.at[2 + i])
        for i, (src, dst) in enumerate(((color_h, color), (opacity_h, opacity), (view_h, view)))
    ]
    for copy in loads:
        copy.start()

    each_z(greet, True)

    @pl.when(g == 0)
    def _():
        zh[0] = jnp.zeros((256, 256), jnp.float32)

    @pl.when(g == 127)
    def _():
        zh[1] = jnp.zeros((256, 256), jnp.float32)

    zero_row = pl.multiple_of(gy * 264, 8)
    dens[:, pl.ds(zero_row, 8), :] = jnp.zeros((2, 8, 256), jnp.float32)

    lane = lax.broadcasted_iota(jnp.int32, (8, 128), 1)
    sub = lax.broadcasted_iota(jnp.int32, (8, 128), 0)

    for copy in loads:
        copy.wait()
    view_rows = view[...].reshape(1, 256)
    flips = [jnp.broadcast_to(view_rows[:, 128 * h:128 * h + 128], (8, 128)) == 1 for h in range(2)]

    load_d.wait()
    edge = pl.multiple_of((1 - gx) * 128, 128)
    packed = jnp.zeros((8, 128), jnp.float32)
    for layer in range(2):
        for t in range(32):
            i = layer * 32 + t
            tile = dens[layer, pl.ds(8 + 8 * t, 8), pl.ds(edge, 128)]
            tile = jnp.where(gx == 0, pltpu.roll(tile, i + 1, 1), pltpu.roll(tile, i, 1))
            packed = jnp.where(lane == i, tile, packed)
    xsend[...] = packed

    load_b.wait()
    tables = jnp.concatenate([color[...].astype(jnp.float32), opacity[...].astype(jnp.float32)], axis=0)
    table = [[jnp.broadcast_to(tables[c:c + 1, 128 * h:128 * h + 128], (8, 128)) for h in range(2)] for c in range(4)]

    def look(entry):
        low = jnp.bitwise_and(entry, 127)
        high = entry >= 128
        return [
            jnp.where(
                high,
                jnp.take_along_axis(table[c][1], low, axis=1, mode="promise_in_bounds"),
                jnp.take_along_axis(table[c][0], low, axis=1, mode="promise_in_bounds"),
            )
            for c in range(4)
        ]

    def lookup_block(s, carry):
        for m in range(4):
            row = pl.multiple_of(32 * s + 8 * m, 8)
            for h in range(2):
                cols = pl.ds(128 * h, 128)
                near = look(bin_v[0, pl.ds(row, 8), cols])
                far = look(bin_v[1, pl.ds(row, 8), cols])
                k_near = jnp.where(flips[h], 1.0 - far[3], 1.0) * near[3]
                k_far = jnp.where(flips[h], 1.0, 1.0 - near[3]) * far[3]
                for c in range(3):
                    coef[c, pl.ds(row, 8), cols] = k_near * near[c]
                    coef[3 + c, pl.ds(row, 8), cols] = k_far * far[c]
                alpha[h, pl.ds(row, 8), :] = near[3] + (1.0 - near[3]) * far[3]
        return carry

    pl.semaphore_wait(
        barrier, 6 + has_prev.astype(jnp.int32) + has_next.astype(jnp.int32) + z)


    def ready(semaphore):
        return lambda target: pl.semaphore_signal(semaphore, inc=1, device_id=target, device_id_type=MESH)

    x_copy = pltpu.make_async_remote_copy(
        src_ref=xsend, dst_ref=xrecv, send_sem=x_s, recv_sem=x_r,
        device_id=(g, gy, 1 - gx), device_id_type=MESH)
    y_from = pl.multiple_of(jnp.where(gy == 0, 256, 8), 8)
    y_to = pl.multiple_of(jnp.where(gy == 0, 0, 264), 8)
    yh_copy = pltpu.make_async_remote_copy(
        src_ref=dens.at[:, pl.ds(y_from, 8), :], dst_ref=dens.at[:, pl.ds(y_to, 8), :],
        send_sem=yh_s, recv_sem=yh_r, device_id=(g, 1 - gy, gx), device_id_type=MESH)

    def z_copy(up, j):
        target = g_next if up else g_prev
        first, count = Z_GROUPS[j]
        rows = 32 * count
        row = 32 * first
        slot = 0 if up else 1
        return pltpu.make_async_remote_copy(
            src_ref=dens.at[1 if up else 0, pl.ds(8 + row, rows), :],
            dst_ref=zh.at[slot, pl.ds(row, rows), :],
            send_sem=zh_s.at[slot, j], recv_sem=zh_r.at[slot, j],
            device_id=(target, gy, gx), device_id_type=MESH)

    def z_start(j):
        pl.when(has_next)(z_copy(True, j).start)
        pl.when(has_prev)(z_copy(False, j).start)

    z_start(0)
    x_copy.start()
    for j in (2, 6):
        ready(y_ready)(at(z, lax.rem(y + j, 8), k))
    yh_copy.start()
    for j in range(1, len(Z_GROUPS)):
        z_start(j)
    lax.fori_loop(0, 8, lookup_block, 0)
    a_copy = pltpu.make_async_remote_copy(
        src_ref=alpha.at[1 - k], dst_ref=arecv, send_sem=a_s, recv_sem=a_r,
        device_id=(sibling, gy, gx), device_id_type=MESH)
    a_copy.start()

    def cut(target, s, m, at_index, value):
        target[(*at_index(2 * m),)] = value[:4]
        target[(*at_index(2 * m + 1),)] = value[4:]

    def pack_alpha(s, carry):
        for m in range(4):
            rows = pl.ds(pl.multiple_of(32 * s + 8 * m, 8), 8)
            own, sib = alpha[k, rows, :], arecv[rows, :]
            cut(asend, s, m, lambda yy: (yy, s), own + (1.0 - own) * sib)
        return carry

    def ya_copy(j, late):
        yy = lax.rem(y + j, 8)
        blocks = pl.ds(4 * late, 4)
        return pltpu.make_async_remote_copy(
            src_ref=asend.at[yy, blocks], dst_ref=yarecv.at[y, blocks],
            send_sem=ya_s.at[late], recv_sem=ya_r.at[late],
            device_id=at(z, yy, k), device_id_type=MESH)

    def ya_wait(buffer, semaphore, late):
        arrived = buffer.at[pl.ds(0, 7), pl.ds(4 * late, 4)]
        pltpu.make_async_copy(arrived, arrived, semaphore.at[late]).wait()

    each_z(ready(z_up), False)

    x_copy.wait_recv()
    columns = xrecv[...]
    for layer in range(2):
        for t in range(32):
            i = layer * 32 + t
            xh[layer, pl.ds(8 * t, 8), :] = jnp.broadcast_to(columns[:, i:i + 1], (8, 128))

    def wait_z(j):
        first, count = Z_GROUPS[j]
        for slot, there in ((0, has_prev), (1, has_next)):
            arrived = zh.at[slot, pl.ds(32 * first, 32 * count), :]
            pl.when(there)(pltpu.make_async_copy(arrived, arrived, zh_r.at[slot, j]).wait)

    def shade_block(s):
        base = pl.multiple_of(32 * s, 32)
        tiles = [[[dens[layer, pl.ds(pl.multiple_of(base + 8 * t, 8), 8), pl.ds(128 * h, 128)] for h in range(2)]
                  for t in range(6)] for layer in range(2)]
        for m in range(4):
            row = pl.multiple_of(base + 8 * m, 8)
            shades = []
            for layer in range(2):
                before, here, after = tiles[layer][m], tiles[layer][m + 1], tiles[layer][m + 2]
                side = xh[layer, pl.ds(row, 8), :]
                ends = [jnp.where(gx == 1, side, 0.0), jnp.where(gx == 0, side, 0.0)]
                to_right = [pltpu.roll(here[h], 1, 1) for h in range(2)]
                to_left = [pltpu.roll(here[h], 127, 1) for h in range(2)]
                left = [jnp.where(lane == 0, ends[0], to_right[0]), jnp.where(lane == 0, to_right[0], to_right[1])]
                right = [jnp.where(lane == 127, to_left[1], to_left[0]), jnp.where(lane == 127, ends[1], to_left[1])]
                for h in range(2):
                    cols = pl.ds(128 * h, 128)
                    above = jnp.where(sub == 0, pltpu.roll(before[h], 1, 0), pltpu.roll(here[h], 1, 0))
                    below = jnp.where(sub == 7, pltpu.roll(after[h], 7, 0), pltpu.roll(here[h], 7, 0))
                    other = tiles[1 - layer][m + 1][h]
                    if layer == 0:
                        dz = other - zh[0, pl.ds(row, 8), cols]
                    else:
                        dz = zh[1, pl.ds(row, 8), cols] - other
                    dx = right[h] - left[h]
                    dy = below - above
                    dot = dx * (0.5 * DIFFUSE * LIGHT_X) + dy * (0.5 * DIFFUSE * LIGHT_Y) + dz * (0.5 * DIFFUSE * LIGHT_Z)
                    norm = 1.0 + 0.25 * (dx * dx + dy * dy + dz * dz)
                    shades.append(AMBIENT + jnp.abs(dot) * lax.rsqrt(norm))
            for h in range(2):
                cols = pl.ds(128 * h, 128)
                for c in range(3):
                    part[s, h, c, pl.ds(8 * m, 8), :] = (
                        coef[c, pl.ds(row, 8), cols] * shades[h] + coef[3 + c, pl.ds(row, 8), cols] * shades[2 + h])

    def d_copy(s):
        return pltpu.make_async_remote_copy(
            src_ref=part.at[s, 1 - k], dst_ref=drecv.at[s], send_sem=d_s.at[s], recv_sem=d_r.at[s],
            device_id=(sibling, gy, gx), device_id_type=MESH)

    flip = jnp.where(k == 0, flips[0].astype(jnp.int32), flips[1].astype(jnp.int32)) == 1
    own_front = jnp.where(flip, 1, 0) == k

    def y_copy(u, first, count, yy):
        blocks = pl.ds(first, count)
        return pltpu.make_async_remote_copy(
            src_ref=ysend.at[yy, blocks], dst_ref=yrecv.at[y, blocks], send_sem=y_s.at[u], recv_sem=y_r.at[u],
            device_id=at(z, yy, k), device_id_type=MESH)

    def y_start(u, first, count):
        for j in (4, 3, 5, 2, 6, 1, 7):
            y_copy(u, first, count, lax.rem(y + j, 8)).start()

    def y_wait(buffer, semaphore, u, first, count):
        arrived = buffer.at[pl.ds(0, 7), pl.ds(first, count)]
        pltpu.make_async_copy(arrived, arrived, semaphore.at[u]).wait()

    def merge_pack(s):
        d_copy(s).wait_recv()
        for m in range(4):
            rows = pl.ds(8 * m, 8)
            whole = pl.ds(pl.multiple_of(32 * s + 8 * m, 8), 8)
            through = 1.0 - jnp.where(own_front, alpha[k, whole, :], arecv[whole, :])
            for c in range(3):
                own, sib = part[s, k, c, rows, :], drecv[s, c, rows, :]
                merged = jnp.where(own_front, own, sib) + through * jnp.where(own_front, sib, own)
                cut(ysend, s, m, lambda yy: (yy, s, c), merged)
        yrecv[y, s] = ysend[y, s]

        for u, (first, count) in enumerate(SENDS):
            @pl.when(s == first + count - 1)
            def _():
                y_start(u, first, count)

    flip4 = flip[:4]

    def weigh(s):
        alphas = [yarecv[i, s] for i in range(8)]
        through = [1.0 - a for a in alphas]
        before, after = [jnp.ones((4, 128), jnp.float32)], [jnp.ones((4, 128), jnp.float32)]
        for i in range(7):
            before.append(before[-1] * through[i])
            after.append(after[-1] * through[7 - i])
        while len(alphas) > 1:
            alphas = [alphas[i] + (1.0 - alphas[i]) * alphas[i + 1] for i in range(0, len(alphas), 2)]
        return [jnp.where(flip4, after[7 - i], before[i]) for i in range(8)], alphas[0]

    def z_send(s):
        @pl.when(s == 0)
        def _():
            ya_wait(yarecv, ya_r, 0)

        @pl.when(s == 4)
        def _():
            ya_wait(yarecv, ya_r, 1)

        weights, whole = weigh(s)

        for u, (first, count) in enumerate(SENDS):
            @pl.when(s == first)
            def _():
                y_wait(yrecv, y_r, u, first, count)

        total = []
        for c in range(3):
            terms = [weights[i] * yrecv[i, s, c] for i in range(8)]
            while len(terms) > 1:
                terms = [terms[i] + terms[i + 1] for i in range(0, len(terms), 2)]
            total.append(terms[0])
        total.append(whole)
        for kk in range(2):
            piece = jnp.concatenate([t[2 * kk:2 * kk + 2] for t in total], axis=0)
            zsend[2 * s + kk] = piece
            mine = jnp.logical_and(s == z, k == kk)

            @pl.when(mine)
            def _():
                zrecv[2 * z + k] = piece

            @pl.when(jnp.logical_not(mine))
            def _():
                pltpu.make_async_remote_copy(
                    src_ref=zsend.at[2 * s + kk], dst_ref=zrecv.at[2 * z + k], send_sem=z_s, recv_sem=z_r,
                    device_id=at(s, y, kk), device_id_type=MESH).start()

    def step(s, carry):
        @pl.when(s == jnp.where(gy == 1, 0, STEPS - 1))
        def _():
            yh_copy.wait_recv()

        for j, (first, _) in enumerate(Z_GROUPS):
            @pl.when(s == first)
            def _():
                wait_z(j)

        @pl.when(s < STEPS)
        def _():
            shade_block(s)
            d_copy(s).start()

        @pl.when(s == 0)
        def _():
            a_copy.wait_recv()
            lax.fori_loop(0, STEPS, pack_alpha, 0)
            yarecv[y] = asend[y]
            for j in (2, 6, 1, 7):
                ya_copy(j, 0).start()
            pl.semaphore_wait(y_ready, 2)
            for j in (4, 3, 5):
                ya_copy(j, 0).start()
            for j in (2, 6, 1, 7):
                ya_copy(j, 1).start()

        @pl.when(jnp.logical_and(s >= SIB_LAG, s < STEPS + SIB_LAG))
        def _():
            merge_pack(s - SIB_LAG)

        @pl.when(s == SIB_LAG + 3)
        def _():
            for j in (4, 3, 5):
                ya_copy(j, 1).start()

        @pl.when(s == LAG - 1)
        def _():
            @pl.when(z < 7)
            def _():
                pl.semaphore_wait(z_up, 7 - z)
            ready(z_both)((sibling, gy, gx))

        @pl.when(s == LAG)
        def _():
            pl.semaphore_wait(z_both, 1)

        @pl.when(s >= LAG)
        def _():
            z_send(s - LAG)
        return carry

    lax.fori_loop(0, STEPS + LAG, step, 0)

    pltpu.make_async_copy(zrecv.at[pl.ds(0, 15)], zrecv.at[pl.ds(0, 15)], z_r).wait()
    for h in range(2):
        level = []
        for i in range(8):
            value = zrecv[2 * i + h]
            spread = jnp.where(sub >= 6, value, pltpu.roll(value, 6, 0))
            spread = jnp.where(sub >= 4, spread, pltpu.roll(spread, 4, 0))
            level.append((value, spread))
        while len(level) > 1:
            merged = []
            for i in range(0, len(level), 2):
                (lv, la), (uv, ua) = level[i], level[i + 1]
                fv, fa = jnp.where(flips[h], uv, lv), jnp.where(flips[h], ua, la)
                bv, ba = jnp.where(flips[h], lv, uv), jnp.where(flips[h], la, ua)
                merged.append((over(fv, fa, bv), over(fa, fa, ba)))
            level = merged
        for c in range(4):
            out[c, :, pl.ds(128 * h, 128)] = level[0][0][2 * c:2 * c + 2, :]

    x_copy.wait_send()
    yh_copy.wait_send()

    for j in range(len(Z_GROUPS)):
        pl.when(has_next)(z_copy(True, j).wait_send)
        pl.when(has_prev)(z_copy(False, j).wait_send)
    a_copy.wait_send()
    for late in range(2):
        ya_wait(asend, ya_s, late)

    def s_drain(s, carry):
        d_copy(s).wait_send()
        return carry

    lax.fori_loop(0, STEPS, s_drain, 0)
    for u, (first, count) in enumerate(SENDS):
        y_wait(ysend, y_s, u, first, count)
    pltpu.make_async_copy(zrecv.at[pl.ds(0, 15)], zrecv.at[pl.ds(0, 15)], z_s).wait()


def local(density, bins, tf_color, tf_opacity, view_back):
    f32 = jnp.float32
    vmem = pl.BlockSpec(memory_space=pltpu.VMEM)
    hbm = pl.BlockSpec(memory_space=pltpu.HBM)
    dma = pltpu.SemaphoreType.DMA
    result = pl.pallas_call(
        kernel,
        out_shape=jax.ShapeDtypeStruct((4, 2, 256), f32),
        in_specs=[hbm] * 5,
        out_specs=vmem,
        scratch_shapes=[
            pltpu.VMEM((3, 256), jnp.bfloat16),
            pltpu.VMEM((1, 256), jnp.bfloat16),
            pltpu.VMEM((256,), jnp.int32),
            pltpu.VMEM((2, 272, 256), f32),
            pltpu.VMEM((2, 256, 256), jnp.int32),
            pltpu.VMEM((6, 256, 256), f32),
            pltpu.VMEM((2, 256, 128), f32),
            pltpu.VMEM((256, 128), f32),
            pltpu.VMEM((8, STEPS, 4, 128), f32),
            pltpu.VMEM((8, STEPS, 4, 128), f32),
            pltpu.VMEM((2, 256, 256), f32),
            pltpu.VMEM((2, 256, 128), f32),
            pltpu.VMEM((8, 128), f32),
            pltpu.VMEM((8, 128), f32),
            pltpu.VMEM((STEPS, 2, 3, 32, 128), f32),
            pltpu.VMEM((STEPS, 3, 32, 128), f32),
            pltpu.VMEM((8, STEPS, 3, 4, 128), f32),
            pltpu.VMEM((8, STEPS, 3, 4, 128), f32),
            pltpu.VMEM((2 * STEPS, 8, 128), f32),
            pltpu.VMEM((16, 8, 128), f32),
            dma((5,)),
            dma((2, 4)),
            dma((2, 4)),
            dma, dma, dma, dma,
            dma((STEPS,)),
            dma((STEPS,)),
            dma((STEPS,)),
            dma((STEPS,)),
            dma, dma, dma, dma,
            dma((2,)),
            dma((2,)),
            pltpu.SemaphoreType.REGULAR,
            pltpu.SemaphoreType.REGULAR,
            pltpu.SemaphoreType.REGULAR,
        ],
        compiler_params=pltpu.CompilerParams(
            collective_id=0, has_side_effects=True, vmem_limit_bytes=60 << 20),
    )(density, bins, tf_color, tf_opacity, view_back)
    return result.reshape(4, 1, 1, 2, 256)


def solution(mesh):
    return jax.shard_map(
        local,
        mesh=mesh,
        in_specs=(P("gz", "gy", "gx"), P("gz", "gy", "gx"), P(), P(), P("gx")),
        out_specs=P(None, "gy", "gz", None, "gx"),
        check_vma=False,
    )
```

```python
import jax
import jax.numpy as jnp
from jax import lax
from jax.experimental import pallas as pl
from jax.experimental.pallas import tpu as pltpu
from jax.sharding import PartitionSpec as P

AMBIENT = 0.2
DIFFUSE = 1.6
LIGHT_X = 0.36
LIGHT_Y = 0.48
LIGHT_Z = 0.8

MESH = pl.DeviceIdType.MESH
STEPS = 8
Z_GROUPS = ((0, 1), (1, 1), (2, 2), (4, 4))
SENDS = ((0, 1), (1, 1), (2, 1), (3, 1), (4, 2), (6, 2))
SIB_LAG = 2
LAG = 7


def over(front, front_alpha, back):
    return front + (1.0 - front_alpha) * back


def kernel(
    density, bins, color_h, opacity_h, view_h, out,
    color, opacity, view, dens, bin_v, coef, alpha, arecv, asend, yarecv, zh, xh, xsend, xrecv, part, drecv, ysend, yrecv, zsend, zrecv,
    in_sem, zh_s, zh_r, x_s, x_r, yh_s, yh_r, d_s, d_r, y_s, y_r, z_s, z_r, a_s, a_r, ya_s, ya_r, y_ready, z_up, z_both,
):
    g = lax.axis_index("gz")
    gy = lax.axis_index("gy")
    gx = lax.axis_index("gx")
    z = lax.div(g, 16)
    y = lax.rem(lax.div(g, 2), 8)
    k = lax.rem(g, 2)
    g_prev = jnp.maximum(g - 1, 0)
    g_next = jnp.minimum(g + 1, 127)
    has_prev = g > 0
    has_next = g < 127
    sibling = g + 1 - 2 * k

    def at(zz, yy, kk):
        return ((zz * 8 + yy) * 2 + kk, gy, gx)

    load_d = pltpu.make_async_copy(density, dens.at[:, pl.ds(8, 256), :], in_sem.at[0])
    load_d.start()
    barrier = pltpu.get_barrier_semaphore()

    def greet(target):
        pl.semaphore_signal(barrier, inc=1, device_id=target, device_id_type=MESH)

    def each_z(do, above):
        for j in range(1, 8):
            zz = z + j if above else z - j

            @pl.when(zz <= 7 if above else zz >= 0)
            def _():
                do(at(zz, y, k))

    greet((g, 1 - gy, gx))
    pl.when(has_prev)(lambda: greet((g_prev, gy, gx)))
    pl.when(has_next)(lambda: greet((g_next, gy, gx)))
    greet((g, gy, 1 - gx))
    for j in (2, 6, 1, 7):
        greet(at(z, lax.rem(y + j, 8), k))
    load_b = pltpu.make_async_copy(bins, bin_v, in_sem.at[1])
    load_b.start()
    loads = [
        pltpu.make_async_copy(src, dst, in_sem.at[2 + i])
        for i, (src, dst) in enumerate(((color_h, color), (opacity_h, opacity), (view_h, view)))
    ]
    for copy in loads:
        copy.start()

    each_z(greet, True)

    @pl.when(g == 0)
    def _():
        zh[0] = jnp.zeros((256, 256), jnp.float32)

    @pl.when(g == 127)
    def _():
        zh[1] = jnp.zeros((256, 256), jnp.float32)

    zero_row = pl.multiple_of(gy * 264, 8)
    dens[:, pl.ds(zero_row, 8), :] = jnp.zeros((2, 8, 256), jnp.float32)

    lane = lax.broadcasted_iota(jnp.int32, (8, 128), 1)
    sub = lax.broadcasted_iota(jnp.int32, (8, 128), 0)

    for copy in loads:
        copy.wait()
    view_rows = view[...].reshape(1, 256)
    flips = [jnp.broadcast_to(view_rows[:, 128 * h:128 * h + 128], (8, 128)) == 1 for h in range(2)]

    load_d.wait()
    edge = pl.multiple_of((1 - gx) * 128, 128)
    packed = jnp.zeros((8, 128), jnp.float32)
    for layer in range(2):
        for t in range(32):
            i = layer * 32 + t
            tile = dens[layer, pl.ds(8 + 8 * t, 8), pl.ds(edge, 128)]
            tile = jnp.where(gx == 0, pltpu.roll(tile, i + 1, 1), pltpu.roll(tile, i, 1))
            packed = jnp.where(lane == i, tile, packed)
    xsend[...] = packed

    load_b.wait()
    tables = jnp.concatenate([color[...].astype(jnp.float32), opacity[...].astype(jnp.float32)], axis=0)
    table = [[jnp.broadcast_to(tables[c:c + 1, 128 * h:128 * h + 128], (8, 128)) for h in range(2)] for c in range(4)]

    def look(entry):
        low = jnp.bitwise_and(entry, 127)
        high = entry >= 128
        return [
            jnp.where(
                high,
                jnp.take_along_axis(table[c][1], low, axis=1, mode="promise_in_bounds"),
                jnp.take_along_axis(table[c][0], low, axis=1, mode="promise_in_bounds"),
            )
            for c in range(4)
        ]

    def lookup_block(s, carry):
        for m in range(4):
            row = pl.multiple_of(32 * s + 8 * m, 8)
            for h in range(2):
                cols = pl.ds(128 * h, 128)
                near = look(bin_v[0, pl.ds(row, 8), cols])
                far = look(bin_v[1, pl.ds(row, 8), cols])
                k_near = jnp.where(flips[h], 1.0 - far[3], 1.0) * near[3]
                k_far = jnp.where(flips[h], 1.0, 1.0 - near[3]) * far[3]
                for c in range(3):
                    coef[c, pl.ds(row, 8), cols] = k_near * near[c]
                    coef[3 + c, pl.ds(row, 8), cols] = k_far * far[c]
                alpha[h, pl.ds(row, 8), :] = near[3] + (1.0 - near[3]) * far[3]
        return carry

    pl.semaphore_wait(
        barrier, 6 + has_prev.astype(jnp.int32) + has_next.astype(jnp.int32) + z)


    def ready(semaphore):
        return lambda target: pl.semaphore_signal(semaphore, inc=1, device_id=target, device_id_type=MESH)

    x_copy = pltpu.make_async_remote_copy(
        src_ref=xsend, dst_ref=xrecv, send_sem=x_s, recv_sem=x_r,
        device_id=(g, gy, 1 - gx), device_id_type=MESH)
    y_from = pl.multiple_of(jnp.where(gy == 0, 256, 8), 8)
    y_to = pl.multiple_of(jnp.where(gy == 0, 0, 264), 8)
    yh_copy = pltpu.make_async_remote_copy(
        src_ref=dens.at[:, pl.ds(y_from, 8), :], dst_ref=dens.at[:, pl.ds(y_to, 8), :],
        send_sem=yh_s, recv_sem=yh_r, device_id=(g, 1 - gy, gx), device_id_type=MESH)

    def z_copy(up, j):
        target = g_next if up else g_prev
        first, count = Z_GROUPS[j]
        rows = 32 * count
        row = 32 * first
        slot = 0 if up else 1
        return pltpu.make_async_remote_copy(
            src_ref=dens.at[1 if up else 0, pl.ds(8 + row, rows), :],
            dst_ref=zh.at[slot, pl.ds(row, rows), :],
            send_sem=zh_s.at[slot, j], recv_sem=zh_r.at[slot, j],
            device_id=(target, gy, gx), device_id_type=MESH)

    def z_start(j):
        pl.when(has_next)(z_copy(True, j).start)
        pl.when(has_prev)(z_copy(False, j).start)

    pl.when(jnp.logical_and(has_next, k == 1))(z_copy(True, 0).start)
    pl.when(jnp.logical_and(has_prev, k == 0))(z_copy(False, 0).start)
    x_copy.start()
    pl.when(k == 0)(z_copy(True, 0).start)
    pl.when(k == 1)(z_copy(False, 0).start)
    for j in (2, 6):
        ready(y_ready)(at(z, lax.rem(y + j, 8), k))
    yh_copy.start()
    for j in range(1, len(Z_GROUPS)):
        z_start(j)
    lax.fori_loop(0, 8, lookup_block, 0)
    a_copy = pltpu.make_async_remote_copy(
        src_ref=alpha.at[1 - k], dst_ref=arecv, send_sem=a_s, recv_sem=a_r,
        device_id=(sibling, gy, gx), device_id_type=MESH)
    a_copy.start()

    def cut(target, s, m, at_index, value):
        target[(*at_index(2 * m),)] = value[:4]
        target[(*at_index(2 * m + 1),)] = value[4:]

    def pack_alpha(s, carry):
        for m in range(4):
            rows = pl.ds(pl.multiple_of(32 * s + 8 * m, 8), 8)
            own, sib = alpha[k, rows, :], arecv[rows, :]
            cut(asend, s, m, lambda yy: (yy, s), own + (1.0 - own) * sib)
        return carry

    def ya_copy(j, late):
        yy = lax.rem(y + j, 8)
        blocks = pl.ds(4 * late, 4)
        return pltpu.make_async_remote_copy(
            src_ref=asend.at[yy, blocks], dst_ref=yarecv.at[y, blocks],
            send_sem=ya_s.at[late], recv_sem=ya_r.at[late],
            device_id=at(z, yy, k), device_id_type=MESH)

    def ya_wait(buffer, semaphore, late):
        arrived = buffer.at[pl.ds(0, 7), pl.ds(4 * late, 4)]
        pltpu.make_async_copy(arrived, arrived, semaphore.at[late]).wait()


    x_copy.wait_recv()
    columns = xrecv[...]
    for layer in range(2):
        for t in range(32):
            i = layer * 32 + t
            xh[layer, pl.ds(8 * t, 8), :] = jnp.broadcast_to(columns[:, i:i + 1], (8, 128))

    def wait_z(j):
        first, count = Z_GROUPS[j]
        for slot, there in ((0, has_prev), (1, has_next)):
            arrived = zh.at[slot, pl.ds(32 * first, 32 * count), :]
            pl.when(there)(pltpu.make_async_copy(arrived, arrived, zh_r.at[slot, j]).wait)

    def shade_block(s):
        base = pl.multiple_of(32 * s, 32)
        tiles = [[[dens[layer, pl.ds(pl.multiple_of(base + 8 * t, 8), 8), pl.ds(128 * h, 128)] for h in range(2)]
                  for t in range(6)] for layer in range(2)]
        for m in range(4):
            row = pl.multiple_of(base + 8 * m, 8)
            shades = []
            for layer in range(2):
                before, here, after = tiles[layer][m], tiles[layer][m + 1], tiles[layer][m + 2]
                side = xh[layer, pl.ds(row, 8), :]
                ends = [jnp.where(gx == 1, side, 0.0), jnp.where(gx == 0, side, 0.0)]
                to_right = [pltpu.roll(here[h], 1, 1) for h in range(2)]
                to_left = [pltpu.roll(here[h], 127, 1) for h in range(2)]
                left = [jnp.where(lane == 0, ends[0], to_right[0]), jnp.where(lane == 0, to_right[0], to_right[1])]
                right = [jnp.where(lane == 127, to_left[1], to_left[0]), jnp.where(lane == 127, ends[1], to_left[1])]
                for h in range(2):
                    cols = pl.ds(128 * h, 128)
                    above = jnp.where(sub == 0, pltpu.roll(before[h], 1, 0), pltpu.roll(here[h], 1, 0))
                    below = jnp.where(sub == 7, pltpu.roll(after[h], 7, 0), pltpu.roll(here[h], 7, 0))
                    other = tiles[1 - layer][m + 1][h]
                    if layer == 0:
                        dz = other - zh[0, pl.ds(row, 8), cols]
                    else:
                        dz = zh[1, pl.ds(row, 8), cols] - other
                    dx = right[h] - left[h]
                    dy = below - above
                    dot = dx * (0.5 * DIFFUSE * LIGHT_X) + dy * (0.5 * DIFFUSE * LIGHT_Y) + dz * (0.5 * DIFFUSE * LIGHT_Z)
                    norm = 1.0 + 0.25 * (dx * dx + dy * dy + dz * dz)
                    shades.append(AMBIENT + jnp.abs(dot) * lax.rsqrt(norm))
            for h in range(2):
                cols = pl.ds(128 * h, 128)
                for c in range(3):
                    part[s, h, c, pl.ds(8 * m, 8), :] = (
                        coef[c, pl.ds(row, 8), cols] * shades[h] + coef[3 + c, pl.ds(row, 8), cols] * shades[2 + h])

    def d_copy(s):
        return pltpu.make_async_remote_copy(
            src_ref=part.at[s, 1 - k], dst_ref=drecv.at[s], send_sem=d_s.at[s], recv_sem=d_r.at[s],
            device_id=(sibling, gy, gx), device_id_type=MESH)

    flip = jnp.where(k == 0, flips[0].astype(jnp.int32), flips[1].astype(jnp.int32)) == 1
    own_front = jnp.where(flip, 1, 0) == k

    def y_copy(u, first, count, yy):
        blocks = pl.ds(first, count)
        return pltpu.make_async_remote_copy(
            src_ref=ysend.at[yy, blocks], dst_ref=yrecv.at[y, blocks], send_sem=y_s.at[u], recv_sem=y_r.at[u],
            device_id=at(z, yy, k), device_id_type=MESH)

    def y_start(u, first, count):
        for j in (4, 3, 5, 2, 6, 1, 7):
            y_copy(u, first, count, lax.rem(y + j, 8)).start()

    def y_wait(buffer, semaphore, u, first, count):
        arrived = buffer.at[pl.ds(0, 7), pl.ds(first, count)]
        pltpu.make_async_copy(arrived, arrived, semaphore.at[u]).wait()

    def merge_pack(s):
        d_copy(s).wait_recv()
        for m in range(4):
            rows = pl.ds(8 * m, 8)
            whole = pl.ds(pl.multiple_of(32 * s + 8 * m, 8), 8)
            through = 1.0 - jnp.where(own_front, alpha[k, whole, :], arecv[whole, :])
            for c in range(3):
                own, sib = part[s, k, c, rows, :], drecv[s, c, rows, :]
                merged = jnp.where(own_front, own, sib) + through * jnp.where(own_front, sib, own)
                cut(ysend, s, m, lambda yy: (yy, s, c), merged)
        yrecv[y, s] = ysend[y, s]

        for u, (first, count) in enumerate(SENDS):
            @pl.when(s == first + count - 1)
            def _():
                y_start(u, first, count)

    flip4 = flip[:4]

    def weigh(s):
        alphas = [yarecv[i, s] for i in range(8)]
        through = [1.0 - a for a in alphas]
        before, after = [jnp.ones((4, 128), jnp.float32)], [jnp.ones((4, 128), jnp.float32)]
        for i in range(7):
            before.append(before[-1] * through[i])
            after.append(after[-1] * through[7 - i])
        while len(alphas) > 1:
            alphas = [alphas[i] + (1.0 - alphas[i]) * alphas[i + 1] for i in range(0, len(alphas), 2)]
        return [jnp.where(flip4, after[7 - i], before[i]) for i in range(8)], alphas[0]

    def z_send(s):
        @pl.when(s == 0)
        def _():
            ya_wait(yarecv, ya_r, 0)

        @pl.when(s == 4)
        def _():
            ya_wait(yarecv, ya_r, 1)

        weights, whole = weigh(s)

        for u, (first, count) in enumerate(SENDS):
            @pl.when(s == first)
            def _():
                y_wait(yrecv, y_r, u, first, count)

        total = []
        for c in range(3):
            terms = [weights[i] * yrecv[i, s, c] for i in range(8)]
            while len(terms) > 1:
                terms = [terms[i] + terms[i + 1] for i in range(0, len(terms), 2)]
            total.append(terms[0])
        total.append(whole)
        for kk in range(2):
            piece = jnp.concatenate([t[2 * kk:2 * kk + 2] for t in total], axis=0)
            zsend[2 * s + kk] = piece
            mine = jnp.logical_and(s == z, k == kk)

            @pl.when(mine)
            def _():
                zrecv[2 * z + k] = piece

            @pl.when(jnp.logical_not(mine))
            def _():
                pltpu.make_async_remote_copy(
                    src_ref=zsend.at[2 * s + kk], dst_ref=zrecv.at[2 * z + k], send_sem=z_s, recv_sem=z_r,
                    device_id=at(s, y, kk), device_id_type=MESH).start()

    def step(s, carry):
        @pl.when(s == jnp.where(gy == 1, 0, STEPS - 1))
        def _():
            yh_copy.wait_recv()

        for j, (first, _) in enumerate(Z_GROUPS):
            @pl.when(s == first)
            def _():
                wait_z(j)

        @pl.when(s < STEPS)
        def _():
            shade_block(s)
            d_copy(s).start()

        @pl.when(s == 0)
        def _():
            each_z(ready(z_up), False)
            a_copy.wait_recv()
            lax.fori_loop(0, STEPS, pack_alpha, 0)
            yarecv[y] = asend[y]
            for j in (2, 6, 1, 7):
                ya_copy(j, 0).start()
            pl.semaphore_wait(y_ready, 2)
            for j in (4, 3, 5):
                ya_copy(j, 0).start()
            for j in (2, 6, 1, 7):
                ya_copy(j, 1).start()

        @pl.when(jnp.logical_and(s >= SIB_LAG, s < STEPS + SIB_LAG))
        def _():
            merge_pack(s - SIB_LAG)

        @pl.when(s == SIB_LAG + 3)
        def _():
            for j in (4, 3, 5):
                ya_copy(j, 1).start()

        @pl.when(s == LAG - 1)
        def _():
            @pl.when(z < 7)
            def _():
                pl.semaphore_wait(z_up, 7 - z)
            ready(z_both)((sibling, gy, gx))

        @pl.when(s == LAG)
        def _():
            pl.semaphore_wait(z_both, 1)

        @pl.when(s >= LAG)
        def _():
            z_send(s - LAG)
        return carry

    lax.fori_loop(0, STEPS + LAG, step, 0)

    pltpu.make_async_copy(zrecv.at[pl.ds(0, 15)], zrecv.at[pl.ds(0, 15)], z_r).wait()
    for h in range(2):
        level = []
        for i in range(8):
            value = zrecv[2 * i + h]
            spread = jnp.where(sub >= 6, value, pltpu.roll(value, 6, 0))
            spread = jnp.where(sub >= 4, spread, pltpu.roll(spread, 4, 0))
            level.append((value, spread))
        while len(level) > 1:
            merged = []
            for i in range(0, len(level), 2):
                (lv, la), (uv, ua) = level[i], level[i + 1]
                fv, fa = jnp.where(flips[h], uv, lv), jnp.where(flips[h], ua, la)
                bv, ba = jnp.where(flips[h], lv, uv), jnp.where(flips[h], la, ua)
                merged.append((over(fv, fa, bv), over(fa, fa, ba)))
            level = merged
        for c in range(4):
            out[c, :, pl.ds(128 * h, 128)] = level[0][0][2 * c:2 * c + 2, :]

    x_copy.wait_send()
    yh_copy.wait_send()

    for j in range(len(Z_GROUPS)):
        pl.when(has_next)(z_copy(True, j).wait_send)
        pl.when(has_prev)(z_copy(False, j).wait_send)
    a_copy.wait_send()
    for late in range(2):
        ya_wait(asend, ya_s, late)

    def s_drain(s, carry):
        d_copy(s).wait_send()
        return carry

    lax.fori_loop(0, STEPS, s_drain, 0)
    for u, (first, count) in enumerate(SENDS):
        y_wait(ysend, y_s, u, first, count)
    pltpu.make_async_copy(zrecv.at[pl.ds(0, 15)], zrecv.at[pl.ds(0, 15)], z_s).wait()


def local(density, bins, tf_color, tf_opacity, view_back):
    f32 = jnp.float32
    vmem = pl.BlockSpec(memory_space=pltpu.VMEM)
    hbm = pl.BlockSpec(memory_space=pltpu.HBM)
    dma = pltpu.SemaphoreType.DMA
    result = pl.pallas_call(
        kernel,
        out_shape=jax.ShapeDtypeStruct((4, 2, 256), f32),
        in_specs=[hbm] * 5,
        out_specs=vmem,
        scratch_shapes=[
            pltpu.VMEM((3, 256), jnp.bfloat16),
            pltpu.VMEM((1, 256), jnp.bfloat16),
            pltpu.VMEM((256,), jnp.int32),
            pltpu.VMEM((2, 272, 256), f32),
            pltpu.VMEM((2, 256, 256), jnp.int32),
            pltpu.VMEM((6, 256, 256), f32),
            pltpu.VMEM((2, 256, 128), f32),
            pltpu.VMEM((256, 128), f32),
            pltpu.VMEM((8, STEPS, 4, 128), f32),
            pltpu.VMEM((8, STEPS, 4, 128), f32),
            pltpu.VMEM((2, 256, 256), f32),
            pltpu.VMEM((2, 256, 128), f32),
            pltpu.VMEM((8, 128), f32),
            pltpu.VMEM((8, 128), f32),
            pltpu.VMEM((STEPS, 2, 3, 32, 128), f32),
            pltpu.VMEM((STEPS, 3, 32, 128), f32),
            pltpu.VMEM((8, STEPS, 3, 4, 128), f32),
            pltpu.VMEM((8, STEPS, 3, 4, 128), f32),
            pltpu.VMEM((2 * STEPS, 8, 128), f32),
            pltpu.VMEM((16, 8, 128), f32),
            dma((5,)),
            dma((2, 4)),
            dma((2, 4)),
            dma, dma, dma, dma,
            dma((STEPS,)),
            dma((STEPS,)),
            dma((STEPS,)),
            dma((STEPS,)),
            dma, dma, dma, dma,
            dma((2,)),
            dma((2,)),
            pltpu.SemaphoreType.REGULAR,
            pltpu.SemaphoreType.REGULAR,
            pltpu.SemaphoreType.REGULAR,
        ],
        compiler_params=pltpu.CompilerParams(
            collective_id=0, has_side_effects=True, vmem_limit_bytes=60 << 20),
    )(density, bins, tf_color, tf_opacity, view_back)
    return result.reshape(4, 1, 1, 2, 256)


def solution(mesh):
    return jax.shard_map(
        local,
        mesh=mesh,
        in_specs=(P("gz", "gy", "gx"), P("gz", "gy", "gx"), P(), P(), P("gx")),
        out_specs=P(None, "gy", "gz", None, "gx"),
        check_vma=False,
    )
```

```python
import jax
import jax.numpy as jnp
from jax import lax
from jax.experimental import pallas as pl
from jax.experimental.pallas import tpu as pltpu
from jax.sharding import PartitionSpec as P

AMBIENT = 0.2
DIFFUSE = 1.6
LIGHT_X = 0.36
LIGHT_Y = 0.48
LIGHT_Z = 0.8

MESH = pl.DeviceIdType.MESH
STEPS = 8
Z_GROUPS = ((0, 1), (1, 1), (2, 2), (4, 4))
SENDS = ((0, 1), (1, 1), (2, 1), (3, 1), (4, 2), (6, 2))
SIB_LAG = 1
LAG = 8


def over(front, front_alpha, back):
    return front + (1.0 - front_alpha) * back


def kernel(
    density, bins, color_h, opacity_h, view_h, out,
    color, opacity, view, dens, bin_v, coef, alpha, arecv, asend, yarecv, zh, xh, xsend, xrecv, part, drecv, ysend, yrecv, zsend, zrecv,
    in_sem, zh_s, zh_r, x_s, x_r, yh_s, yh_r, d_s, d_r, y_s, y_r, z_s, z_r, a_s, a_r, ya_s, ya_r, y_ready, z_up, z_both,
):
    g = lax.axis_index("gz")
    gy = lax.axis_index("gy")
    gx = lax.axis_index("gx")
    z = lax.div(g, 16)
    y = lax.rem(lax.div(g, 2), 8)
    k = lax.rem(g, 2)
    g_prev = jnp.maximum(g - 1, 0)
    g_next = jnp.minimum(g + 1, 127)
    has_prev = g > 0
    has_next = g < 127
    sibling = g + 1 - 2 * k

    def at(zz, yy, kk):
        return ((zz * 8 + yy) * 2 + kk, gy, gx)

    load_d = pltpu.make_async_copy(density, dens.at[:, pl.ds(8, 256), :], in_sem.at[0])
    load_d.start()
    barrier = pltpu.get_barrier_semaphore()

    def greet(target):
        pl.semaphore_signal(barrier, inc=1, device_id=target, device_id_type=MESH)

    def each_z(do, above):
        for j in range(1, 8):
            zz = z + j if above else z - j

            @pl.when(zz <= 7 if above else zz >= 0)
            def _():
                do(at(zz, y, k))

    greet((g, 1 - gy, gx))
    pl.when(has_prev)(lambda: greet((g_prev, gy, gx)))
    pl.when(has_next)(lambda: greet((g_next, gy, gx)))
    greet((g, gy, 1 - gx))
    for j in (2, 6, 1, 7):
        greet(at(z, lax.rem(y + j, 8), k))
    load_b = pltpu.make_async_copy(bins, bin_v, in_sem.at[1])
    load_b.start()
    loads = [
        pltpu.make_async_copy(src, dst, in_sem.at[2 + i])
        for i, (src, dst) in enumerate(((color_h, color), (opacity_h, opacity), (view_h, view)))
    ]
    for copy in loads:
        copy.start()

    each_z(greet, True)

    @pl.when(g == 0)
    def _():
        zh[0] = jnp.zeros((256, 256), jnp.float32)

    @pl.when(g == 127)
    def _():
        zh[1] = jnp.zeros((256, 256), jnp.float32)

    zero_row = pl.multiple_of(gy * 264, 8)
    dens[:, pl.ds(zero_row, 8), :] = jnp.zeros((2, 8, 256), jnp.float32)

    lane = lax.broadcasted_iota(jnp.int32, (8, 128), 1)
    sub = lax.broadcasted_iota(jnp.int32, (8, 128), 0)

    for copy in loads:
        copy.wait()
    view_rows = view[...].reshape(1, 256)
    flips = [jnp.broadcast_to(view_rows[:, 128 * h:128 * h + 128], (8, 128)) == 1 for h in range(2)]

    load_d.wait()
    edge = pl.multiple_of((1 - gx) * 128, 128)
    packed = jnp.zeros((8, 128), jnp.float32)
    for layer in range(2):
        for t in range(32):
            i = layer * 32 + t
            tile = dens[layer, pl.ds(8 + 8 * t, 8), pl.ds(edge, 128)]
            tile = jnp.where(gx == 0, pltpu.roll(tile, i + 1, 1), pltpu.roll(tile, i, 1))
            packed = jnp.where(lane == i, tile, packed)
    xsend[...] = packed

    load_b.wait()
    tables = jnp.concatenate([color[...].astype(jnp.float32), opacity[...].astype(jnp.float32)], axis=0)
    table = [[jnp.broadcast_to(tables[c:c + 1, 128 * h:128 * h + 128], (8, 128)) for h in range(2)] for c in range(4)]

    def look(entry):
        low = jnp.bitwise_and(entry, 127)
        high = entry >= 128
        return [
            jnp.where(
                high,
                jnp.take_along_axis(table[c][1], low, axis=1, mode="promise_in_bounds"),
                jnp.take_along_axis(table[c][0], low, axis=1, mode="promise_in_bounds"),
            )
            for c in range(4)
        ]

    def lookup_block(s, carry):
        for m in range(4):
            row = pl.multiple_of(32 * s + 8 * m, 8)
            for h in range(2):
                cols = pl.ds(128 * h, 128)
                near = look(bin_v[0, pl.ds(row, 8), cols])
                far = look(bin_v[1, pl.ds(row, 8), cols])
                k_near = jnp.where(flips[h], 1.0 - far[3], 1.0) * near[3]
                k_far = jnp.where(flips[h], 1.0, 1.0 - near[3]) * far[3]
                for c in range(3):
                    coef[c, pl.ds(row, 8), cols] = k_near * near[c]
                    coef[3 + c, pl.ds(row, 8), cols] = k_far * far[c]
                alpha[h, pl.ds(row, 8), :] = near[3] + (1.0 - near[3]) * far[3]
        return carry

    pl.semaphore_wait(
        barrier, 6 + has_prev.astype(jnp.int32) + has_next.astype(jnp.int32) + z)


    def ready(semaphore):
        return lambda target: pl.semaphore_signal(semaphore, inc=1, device_id=target, device_id_type=MESH)

    x_copy = pltpu.make_async_remote_copy(
        src_ref=xsend, dst_ref=xrecv, send_sem=x_s, recv_sem=x_r,
        device_id=(g, gy, 1 - gx), device_id_type=MESH)
    y_from = pl.multiple_of(jnp.where(gy == 0, 256, 8), 8)
    y_to = pl.multiple_of(jnp.where(gy == 0, 0, 264), 8)
    yh_copy = pltpu.make_async_remote_copy(
        src_ref=dens.at[:, pl.ds(y_from, 8), :], dst_ref=dens.at[:, pl.ds(y_to, 8), :],
        send_sem=yh_s, recv_sem=yh_r, device_id=(g, 1 - gy, gx), device_id_type=MESH)

    def z_copy(up, j):
        target = g_next if up else g_prev
        first, count = Z_GROUPS[j]
        rows = 32 * count
        row = 32 * first
        slot = 0 if up else 1
        return pltpu.make_async_remote_copy(
            src_ref=dens.at[1 if up else 0, pl.ds(8 + row, rows), :],
            dst_ref=zh.at[slot, pl.ds(row, rows), :],
            send_sem=zh_s.at[slot, j], recv_sem=zh_r.at[slot, j],
            device_id=(target, gy, gx), device_id_type=MESH)

    def z_start(j):
        pl.when(has_next)(z_copy(True, j).start)
        pl.when(has_prev)(z_copy(False, j).start)

    z_start(0)
    x_copy.start()
    for j in (2, 6):
        ready(y_ready)(at(z, lax.rem(y + j, 8), k))
    yh_copy.start()
    for j in range(1, len(Z_GROUPS)):
        z_start(j)
    lax.fori_loop(0, 8, lookup_block, 0)
    a_copy = pltpu.make_async_remote_copy(
        src_ref=alpha.at[1 - k], dst_ref=arecv, send_sem=a_s, recv_sem=a_r,
        device_id=(sibling, gy, gx), device_id_type=MESH)
    a_copy.start()

    def cut(target, s, m, at_index, value):
        target[(*at_index(2 * m),)] = value[:4]
        target[(*at_index(2 * m + 1),)] = value[4:]

    def pack_alpha(s, carry):
        for m in range(4):
            rows = pl.ds(pl.multiple_of(32 * s + 8 * m, 8), 8)
            own, sib = alpha[k, rows, :], arecv[rows, :]
            cut(asend, s, m, lambda yy: (yy, s), own + (1.0 - own) * sib)
        return carry

    def ya_copy(j, late):
        yy = lax.rem(y + j, 8)
        blocks = pl.ds(4 * late, 4)
        return pltpu.make_async_remote_copy(
            src_ref=asend.at[yy, blocks], dst_ref=yarecv.at[y, blocks],
            send_sem=ya_s.at[late], recv_sem=ya_r.at[late],
            device_id=at(z, yy, k), device_id_type=MESH)

    def ya_wait(buffer, semaphore, late):
        arrived = buffer.at[pl.ds(0, 7), pl.ds(4 * late, 4)]
        pltpu.make_async_copy(arrived, arrived, semaphore.at[late]).wait()

    each_z(ready(z_up), False)

    x_copy.wait_recv()
    columns = xrecv[...]
    for layer in range(2):
        for t in range(32):
            i = layer * 32 + t
            xh[layer, pl.ds(8 * t, 8), :] = jnp.broadcast_to(columns[:, i:i + 1], (8, 128))

    def wait_z(j):
        first, count = Z_GROUPS[j]
        for slot, there in ((0, has_prev), (1, has_next)):
            arrived = zh.at[slot, pl.ds(32 * first, 32 * count), :]
            pl.when(there)(pltpu.make_async_copy(arrived, arrived, zh_r.at[slot, j]).wait)

    def shade_block(s):
        base = pl.multiple_of(32 * s, 32)
        tiles = [[[dens[layer, pl.ds(pl.multiple_of(base + 8 * t, 8), 8), pl.ds(128 * h, 128)] for h in range(2)]
                  for t in range(6)] for layer in range(2)]
        for m in range(4):
            row = pl.multiple_of(base + 8 * m, 8)
            shades = []
            for layer in range(2):
                before, here, after = tiles[layer][m], tiles[layer][m + 1], tiles[layer][m + 2]
                side = xh[layer, pl.ds(row, 8), :]
                ends = [jnp.where(gx == 1, side, 0.0), jnp.where(gx == 0, side, 0.0)]
                to_right = [pltpu.roll(here[h], 1, 1) for h in range(2)]
                to_left = [pltpu.roll(here[h], 127, 1) for h in range(2)]
                left = [jnp.where(lane == 0, ends[0], to_right[0]), jnp.where(lane == 0, to_right[0], to_right[1])]
                right = [jnp.where(lane == 127, to_left[1], to_left[0]), jnp.where(lane == 127, ends[1], to_left[1])]
                for h in range(2):
                    cols = pl.ds(128 * h, 128)
                    above = jnp.where(sub == 0, pltpu.roll(before[h], 1, 0), pltpu.roll(here[h], 1, 0))
                    below = jnp.where(sub == 7, pltpu.roll(after[h], 7, 0), pltpu.roll(here[h], 7, 0))
                    other = tiles[1 - layer][m + 1][h]
                    if layer == 0:
                        dz = other - zh[0, pl.ds(row, 8), cols]
                    else:
                        dz = zh[1, pl.ds(row, 8), cols] - other
                    dx = right[h] - left[h]
                    dy = below - above
                    dot = dx * (0.5 * DIFFUSE * LIGHT_X) + dy * (0.5 * DIFFUSE * LIGHT_Y) + dz * (0.5 * DIFFUSE * LIGHT_Z)
                    norm = 1.0 + 0.25 * (dx * dx + dy * dy + dz * dz)
                    shades.append(AMBIENT + jnp.abs(dot) * lax.rsqrt(norm))
            for h in range(2):
                cols = pl.ds(128 * h, 128)
                for c in range(3):
                    part[s, h, c, pl.ds(8 * m, 8), :] = (
                        coef[c, pl.ds(row, 8), cols] * shades[h] + coef[3 + c, pl.ds(row, 8), cols] * shades[2 + h])

    def d_copy(s):
        return pltpu.make_async_remote_copy(
            src_ref=part.at[s, 1 - k], dst_ref=drecv.at[s], send_sem=d_s.at[s], recv_sem=d_r.at[s],
            device_id=(sibling, gy, gx), device_id_type=MESH)

    flip = jnp.where(k == 0, flips[0].astype(jnp.int32), flips[1].astype(jnp.int32)) == 1
    own_front = jnp.where(flip, 1, 0) == k

    def y_copy(u, first, count, yy):
        blocks = pl.ds(first, count)
        return pltpu.make_async_remote_copy(
            src_ref=ysend.at[yy, blocks], dst_ref=yrecv.at[y, blocks], send_sem=y_s.at[u], recv_sem=y_r.at[u],
            device_id=at(z, yy, k), device_id_type=MESH)

    def y_start(u, first, count):
        for j in (4, 3, 5, 2, 6, 1, 7):
            y_copy(u, first, count, lax.rem(y + j, 8)).start()

    def y_wait(buffer, semaphore, u, first, count):
        arrived = buffer.at[pl.ds(0, 7), pl.ds(first, count)]
        pltpu.make_async_copy(arrived, arrived, semaphore.at[u]).wait()

    def merge_pack(s):
        d_copy(s).wait_recv()
        for m in range(4):
            rows = pl.ds(8 * m, 8)
            whole = pl.ds(pl.multiple_of(32 * s + 8 * m, 8), 8)
            through = 1.0 - jnp.where(own_front, alpha[k, whole, :], arecv[whole, :])
            for c in range(3):
                own, sib = part[s, k, c, rows, :], drecv[s, c, rows, :]
                merged = jnp.where(own_front, own, sib) + through * jnp.where(own_front, sib, own)
                cut(ysend, s, m, lambda yy: (yy, s, c), merged)
        yrecv[y, s] = ysend[y, s]

        for u, (first, count) in enumerate(SENDS):
            @pl.when(s == first + count - 1)
            def _():
                y_start(u, first, count)

    flip4 = flip[:4]

    def weigh(s):
        alphas = [yarecv[i, s] for i in range(8)]
        through = [1.0 - a for a in alphas]
        before, after = [jnp.ones((4, 128), jnp.float32)], [jnp.ones((4, 128), jnp.float32)]
        for i in range(7):
            before.append(before[-1] * through[i])
            after.append(after[-1] * through[7 - i])
        while len(alphas) > 1:
            alphas = [alphas[i] + (1.0 - alphas[i]) * alphas[i + 1] for i in range(0, len(alphas), 2)]
        return [jnp.where(flip4, after[7 - i], before[i]) for i in range(8)], alphas[0]

    def z_send(s):
        @pl.when(s == 0)
        def _():
            ya_wait(yarecv, ya_r, 0)

        @pl.when(s == 4)
        def _():
            ya_wait(yarecv, ya_r, 1)

        weights, whole = weigh(s)

        for u, (first, count) in enumerate(SENDS):
            @pl.when(s == first)
            def _():
                y_wait(yrecv, y_r, u, first, count)

        total = []
        for c in range(3):
            terms = [weights[i] * yrecv[i, s, c] for i in range(8)]
            while len(terms) > 1:
                terms = [terms[i] + terms[i + 1] for i in range(0, len(terms), 2)]
            total.append(terms[0])
        total.append(whole)
        for kk in range(2):
            piece = jnp.concatenate([t[2 * kk:2 * kk + 2] for t in total], axis=0)
            zsend[2 * s + kk] = piece
            mine = jnp.logical_and(s == z, k == kk)

            @pl.when(mine)
            def _():
                zrecv[2 * z + k] = piece

            @pl.when(jnp.logical_not(mine))
            def _():
                pltpu.make_async_remote_copy(
                    src_ref=zsend.at[2 * s + kk], dst_ref=zrecv.at[2 * z + k], send_sem=z_s, recv_sem=z_r,
                    device_id=at(s, y, kk), device_id_type=MESH).start()

    def step(s, carry):
        @pl.when(s == jnp.where(gy == 1, 0, STEPS - 1))
        def _():
            yh_copy.wait_recv()

        for j, (first, _) in enumerate(Z_GROUPS):
            @pl.when(s == first)
            def _():
                wait_z(j)

        @pl.when(s < STEPS)
        def _():
            shade_block(s)
            d_copy(s).start()

        @pl.when(s == 0)
        def _():
            a_copy.wait_recv()
            lax.fori_loop(0, 4, pack_alpha, 0)
            yarecv[y, pl.ds(0, 4)] = asend[y, pl.ds(0, 4)]
            for j in (2, 6, 1, 7):
                ya_copy(j, 0).start()
            pl.semaphore_wait(y_ready, 2)
            for j in (4, 3, 5):
                ya_copy(j, 0).start()

        @pl.when(jnp.logical_and(s >= SIB_LAG, s < STEPS + SIB_LAG))
        def _():
            merge_pack(s - SIB_LAG)

        @pl.when(s == SIB_LAG)
        def _():
            lax.fori_loop(4, STEPS, pack_alpha, 0)
            yarecv[y, pl.ds(4, 4)] = asend[y, pl.ds(4, 4)]
            for j in (2, 6, 1, 7):
                ya_copy(j, 1).start()

        @pl.when(s == SIB_LAG + 3)
        def _():
            for j in (4, 3, 5):
                ya_copy(j, 1).start()

        @pl.when(s == LAG - 1)
        def _():
            @pl.when(z < 7)
            def _():
                pl.semaphore_wait(z_up, 7 - z)
            ready(z_both)((sibling, gy, gx))

        @pl.when(s == LAG)
        def _():
            pl.semaphore_wait(z_both, 1)

        @pl.when(s >= LAG)
        def _():
            z_send(s - LAG)
        return carry

    lax.fori_loop(0, STEPS + LAG, step, 0)

    pltpu.make_async_copy(zrecv.at[pl.ds(0, 15)], zrecv.at[pl.ds(0, 15)], z_r).wait()
    for h in range(2):
        level = []
        for i in range(8):
            value = zrecv[2 * i + h]
            spread = jnp.where(sub >= 6, value, pltpu.roll(value, 6, 0))
            spread = jnp.where(sub >= 4, spread, pltpu.roll(spread, 4, 0))
            level.append((value, spread))
        while len(level) > 1:
            merged = []
            for i in range(0, len(level), 2):
                (lv, la), (uv, ua) = level[i], level[i + 1]
                fv, fa = jnp.where(flips[h], uv, lv), jnp.where(flips[h], ua, la)
                bv, ba = jnp.where(flips[h], lv, uv), jnp.where(flips[h], la, ua)
                merged.append((over(fv, fa, bv), over(fa, fa, ba)))
            level = merged
        for c in range(4):
            out[c, :, pl.ds(128 * h, 128)] = level[0][0][2 * c:2 * c + 2, :]

    x_copy.wait_send()
    yh_copy.wait_send()

    for j in range(len(Z_GROUPS)):
        pl.when(has_next)(z_copy(True, j).wait_send)
        pl.when(has_prev)(z_copy(False, j).wait_send)
    a_copy.wait_send()
    for late in range(2):
        ya_wait(asend, ya_s, late)

    def s_drain(s, carry):
        d_copy(s).wait_send()
        return carry

    lax.fori_loop(0, STEPS, s_drain, 0)
    for u, (first, count) in enumerate(SENDS):
        y_wait(ysend, y_s, u, first, count)
    pltpu.make_async_copy(zrecv.at[pl.ds(0, 15)], zrecv.at[pl.ds(0, 15)], z_s).wait()


def local(density, bins, tf_color, tf_opacity, view_back):
    f32 = jnp.float32
    vmem = pl.BlockSpec(memory_space=pltpu.VMEM)
    hbm = pl.BlockSpec(memory_space=pltpu.HBM)
    dma = pltpu.SemaphoreType.DMA
    result = pl.pallas_call(
        kernel,
        out_shape=jax.ShapeDtypeStruct((4, 2, 256), f32),
        in_specs=[hbm] * 5,
        out_specs=vmem,
        scratch_shapes=[
            pltpu.VMEM((3, 256), jnp.bfloat16),
            pltpu.VMEM((1, 256), jnp.bfloat16),
            pltpu.VMEM((256,), jnp.int32),
            pltpu.VMEM((2, 272, 256), f32),
            pltpu.VMEM((2, 256, 256), jnp.int32),
            pltpu.VMEM((6, 256, 256), f32),
            pltpu.VMEM((2, 256, 128), f32),
            pltpu.VMEM((256, 128), f32),
            pltpu.VMEM((8, STEPS, 4, 128), f32),
            pltpu.VMEM((8, STEPS, 4, 128), f32),
            pltpu.VMEM((2, 256, 256), f32),
            pltpu.VMEM((2, 256, 128), f32),
            pltpu.VMEM((8, 128), f32),
            pltpu.VMEM((8, 128), f32),
            pltpu.VMEM((STEPS, 2, 3, 32, 128), f32),
            pltpu.VMEM((STEPS, 3, 32, 128), f32),
            pltpu.VMEM((8, STEPS, 3, 4, 128), f32),
            pltpu.VMEM((8, STEPS, 3, 4, 128), f32),
            pltpu.VMEM((2 * STEPS, 8, 128), f32),
            pltpu.VMEM((16, 8, 128), f32),
            dma((5,)),
            dma((2, 4)),
            dma((2, 4)),
            dma, dma, dma, dma,
            dma((STEPS,)),
            dma((STEPS,)),
            dma((STEPS,)),
            dma((STEPS,)),
            dma, dma, dma, dma,
            dma((2,)),
            dma((2,)),
            pltpu.SemaphoreType.REGULAR,
            pltpu.SemaphoreType.REGULAR,
            pltpu.SemaphoreType.REGULAR,
        ],
        compiler_params=pltpu.CompilerParams(
            collective_id=0, has_side_effects=True, vmem_limit_bytes=60 << 20),
    )(density, bins, tf_color, tf_opacity, view_back)
    return result.reshape(4, 1, 1, 2, 256)


def solution(mesh):
    return jax.shard_map(
        local,
        mesh=mesh,
        in_specs=(P("gz", "gy", "gx"), P("gz", "gy", "gx"), P(), P(), P("gx")),
        out_specs=P(None, "gy", "gz", None, "gx"),
        check_vma=False,
    )
```
